32 devices in a mesh: corpus: 8 (over z, y), vocab: 4 (over x, core).
Axes of the slice: x: 2, y: 2, z: 4, core: 2. Of those that a mesh axis runs over, the one named last changes fastest.
Arguments:
- eval_tiles: bfloat16 [8, 12, 128, 512], P('corpus', 'vocab'), may hold values from 0.019897461 to 2
- eval_tile_list: int32 [8, 12], P(None, 'vocab'), may hold values from 0 to 128, as said below
- corpus_tiles: bfloat16 [32, 12, 128, 512], P('corpus', 'vocab'), may hold values from 0.019897461 to 2
- corpus_tile_list: int32 [32, 12], P('corpus', 'vocab'), may hold values from 0 to 128, as said below
- pair_eval_block: int32 [768], P('corpus'), may hold values from 0 to 7
- pair_corpus_block: int32 [768], P('corpus'), may hold values from 0 to 3
- pair_count: int32 [8], P('corpus'), may hold values from 12 to 96, as said below
- eval_norm: float32 [1024], replicated, may hold values from 8 to 32
- corpus_norm: float32 [4096], P('corpus'), may hold values from 8 to 32
Outputs:
- cosine_tiles: float32 [768, 128, 128], P(('corpus', 'vocab'))
The draws below stay inside these ranges and needn't reach their ends.
Inputs may be any that keep to these rules, and one draw needn't show every extreme that they name: `eval_tile_list`: value 128 marks an empty slot; other ids of one row block in one slice are distinct. Slot 0 of a block and slice is never empty. `corpus_tile_list`: value 128 marks an empty slot; other ids of one row block in one slice are distinct. Slot 0 of a block and slice is never empty. Shard c's live pair slots are its first pair_count[c] slots. Some shard is full.
All inputs are finite; a program needn't handle non-finite values.
Results may differ from the reference program's by a relative error of at most 0.0003.
Values may be sent and summed in bfloat16 or wider, within the bound.
No kernel may reach another device: no remote copies, remote signals or barrier semaphores. Data moves between devices by JAX's collectives and lax.ppermute only.
A program may use at most 128 MiB of HBM per device.

```python
import math
import jax
import jax.numpy as jnp
from jax import lax

TILE_ROWS = 128
TILE_TERMS = 512
SLOTS = 3
DB_DEV = 4
P_DEV = 96
SLICES = 4
SHARDS = 8
TILES_SLICE = 128
EB = 8
DB = 32
EVALS = 1024
DOCS = 4096
PAIRS = 768


def tile_list(key, blocks):
    columns = SLICES * SLOTS
    column = jnp.arange(columns, dtype=jnp.int32)
    slice_of = column // SLOTS
    slot_of = column % SLOTS
    first_key, rest_key, vacant_key = jax.random.split(key, 3)
    frequent = jax.random.randint(first_key, (blocks, columns), 0, 3)
    rare_tiles = 3 + (slot_of - 1) * 2 + jax.random.randint(rest_key, (blocks, columns), 0, 2)
    chosen = jnp.where(slot_of == 0, frequent, rare_tiles)
    vacant = (jax.random.randint(vacant_key, (blocks, columns), 0, 2 * SLICES) < slice_of) & (slot_of > 0)
    block_row = jnp.arange(blocks, dtype=jnp.int32)[:, None]
    forced_vacant = (block_row == 0) & (slice_of == SLICES - 1) & (slot_of == 1)
    chosen = jnp.where(vacant | forced_vacant, TILES_SLICE, chosen)
    chosen = jnp.where((block_row == 0) & (column == 0), 0, chosen)
    return chosen.astype(jnp.int32)


def draw_eval_tile_list(key, part):
    return tile_list(jax.random.fold_in(key, 11), EB)


def draw_corpus_tile_list(key, part):
    return tile_list(jax.random.fold_in(key, 23), DB)


def draw_pair_count(key, part):
    light_key, heavy_key = jax.random.split(jax.random.fold_in(key, 37))
    lighter = jax.random.randint(light_key, (SHARDS,), P_DEV // 8, P_DEV // 2 + 1)
    busiest = jax.random.randint(heavy_key, (), 0, SHARDS)
    return jnp.where(jnp.arange(SHARDS) == busiest, P_DEV, lighter).astype(jnp.int32)


def plant(entries, rng, low, top_value):
    longest = entries.shape.index(max(entries.shape))
    spots = []
    for shift in (0, 1):
        where = [jax.random.randint(jax.random.fold_in(rng, axis), (), 0, length) for axis, length in enumerate(entries.shape)]
        where[longest] = (where[longest] + shift) % entries.shape[longest]
        spots.append(tuple(where))
    return entries.at[spots[0]].set(low).at[spots[1]].set(top_value)


def steps_of(rng, dims, pieces, smallest, largest):
    factor_of, own = 1.0, jax.random.fold_in(rng, 6)
    for axis_at, blocks in pieces:
        draws = jnp.exp(jax.random.uniform(jax.random.fold_in(own, axis_at), (blocks,), jnp.float32, smallest / len(pieces), largest / len(pieces)))
        factor_of = factor_of * jnp.repeat(draws, dims[axis_at] // blocks).reshape([-1 if axis == axis_at else 1 for axis in range(len(dims))])
    return factor_of


def setup_inputs(seed: int = 0) -> dict:
    arg_keys = jax.random.split(jax.random.key(seed), 10)
    eval_tiles = jnp.clip(jnp.exp(math.log(2.0) - 4.61031033 * jax.random.uniform(arg_keys[0], (EB, SLICES * SLOTS, TILE_ROWS, TILE_TERMS), jnp.float32) ** steps_of(arg_keys[0], (EB, SLICES * SLOTS, TILE_ROWS, TILE_TERMS), ((0, 8), (1, 4)), -0.2, 0.2)), 0.019897461, 2.0).astype(jnp.bfloat16)
    eval_tile_list = draw_eval_tile_list(jax.random.fold_in(arg_keys[9], 71), 0)
    corpus_tiles = jnp.clip(jnp.exp(math.log(2.0) - 4.61031033 * jax.random.uniform(arg_keys[2], (DB, SLICES * SLOTS, TILE_ROWS, TILE_TERMS), jnp.float32) ** steps_of(arg_keys[2], (DB, SLICES * SLOTS, TILE_ROWS, TILE_TERMS), ((0, 8), (1, 4)), -0.2, 0.2)), 0.019897461, 2.0).astype(jnp.bfloat16)
    corpus_tile_list = draw_corpus_tile_list(jax.random.fold_in(arg_keys[9], 71), 0)
    pair_eval_block = plant(jax.random.randint(arg_keys[4], (PAIRS,), 0, EB), jax.random.fold_in(arg_keys[4], 1), 0, EB - 1).astype(jnp.int32)
    pair_corpus_block = plant(jax.random.randint(arg_keys[5], (PAIRS,), 0, DB_DEV), jax.random.fold_in(arg_keys[5], 1), 0, DB_DEV - 1).astype(jnp.int32)
    pair_count = draw_pair_count(jax.random.fold_in(arg_keys[9], 71), 0)
    eval_norm = jnp.clip(jnp.exp(jax.random.uniform(arg_keys[7], (EVALS,), jnp.float32, math.log(8.0), math.log(32.0))), 8.0, 32.0)
    corpus_norm = jnp.clip(jnp.exp(math.log(32.0) - 1.3862944 * jax.random.uniform(arg_keys[8], (DOCS,), jnp.float32) ** steps_of(arg_keys[8], (DOCS,), ((0, 8),), -0.2, 0.2)), 8.0, 32.0)
    return {"eval_tiles": eval_tiles, "eval_tile_list": eval_tile_list, "corpus_tiles": corpus_tiles, "corpus_tile_list": corpus_tile_list, "pair_eval_block": pair_eval_block, "pair_corpus_block": pair_corpus_block, "pair_count": pair_count, "eval_norm": eval_norm, "corpus_norm": corpus_norm}


def reference(eval_tiles, eval_tile_list, corpus_tiles, corpus_tile_list, pair_eval_block, pair_corpus_block, pair_count, eval_norm, corpus_norm):
    column = jnp.arange(SLICES * SLOTS, dtype=jnp.int32)
    same_slice = (column[:, None] // SLOTS) == (column[None, :] // SLOTS)
    eval_scale_all = eval_norm.reshape(EB, TILE_ROWS)
    corpus_scale_all = corpus_norm.reshape(DB, TILE_ROWS)

    def one_pair(pair):
        shard_index = pair // P_DEV
        eval_block = pair_eval_block[pair]
        corpus_block = shard_index * DB_DEV + pair_corpus_block[pair]
        eval_list = eval_tile_list[eval_block]
        corpus_list = corpus_tile_list[corpus_block]
        matched = same_slice & (eval_list[:, None] == corpus_list[None, :]) & (eval_list[:, None] < TILES_SLICE)
        eval_part = eval_tiles[eval_block].astype(jnp.float32)
        corpus_part = corpus_tiles[corpus_block].astype(jnp.float32)
        aligned = jnp.einsum("ij,jrt->irt", matched.astype(jnp.float32), corpus_part, precision=lax.Precision.HIGHEST)
        products = jnp.einsum("irt,ist->rs", eval_part, aligned, precision=lax.Precision.HIGHEST)
        cosine = products / (eval_scale_all[eval_block][:, None] * corpus_scale_all[corpus_block][None, :])
        alive_pair = (pair % P_DEV) < pair_count[shard_index]
        return jnp.where(alive_pair, cosine, jnp.zeros_like(cosine))

    batches = jnp.arange(PAIRS, dtype=jnp.int32).reshape(PAIRS // 8, 8)
    result = lax.map(jax.vmap(one_pair), batches)
    return result.reshape(PAIRS, TILE_ROWS, TILE_ROWS)
```

```python
import functools

import jax
import jax.numpy as jnp
from jax import lax
from jax.experimental import pallas as pl
from jax.experimental.pallas import tpu as pltpu
from jax.sharding import PartitionSpec as P

VOCAB = 262144
GROUP = 8
VMEM = pl.BlockSpec(memory_space=pltpu.VMEM)
SMEM = pl.BlockSpec(memory_space=pltpu.SMEM)
LIMIT = 24 * 1024 * 1024


def tiles_in_slice(corpus_tiles):
    return VOCAB // (corpus_tiles.shape[3] * lax.axis_size("vocab"))


def general(
    eval_tiles,
    eval_tile_list,
    corpus_tiles,
    corpus_tile_list,
    pair_eval_block,
    pair_corpus_block,
    pair_count,
    eval_norm,
    corpus_norm,
):
    slices = lax.axis_size("vocab")
    tile_rows = corpus_tiles.shape[2]
    tiles_slice = tiles_in_slice(corpus_tiles)
    pair_slots = pair_eval_block.shape[0]
    quarter = pair_slots // slices
    every_eval = lax.all_gather(eval_tiles, "corpus", axis=0, tiled=True)
    position = jnp.arange(pair_slots, dtype=jnp.int32)
    own_live = position < pair_count[0]
    groups = pair_slots // GROUP

    def one_group(group_index, totals):
        first_slot = group_index * GROUP
        living = lax.dynamic_slice_in_dim(own_live, first_slot, GROUP)

        def compute(current):
            eval_index = lax.dynamic_slice_in_dim(pair_eval_block, first_slot, GROUP)
            block_index = lax.dynamic_slice_in_dim(pair_corpus_block, first_slot, GROUP)
            eval_part = every_eval[eval_index]
            eval_list = eval_tile_list[eval_index]
            corpus_part = corpus_tiles[block_index]
            corpus_list = corpus_tile_list[block_index]
            matched = (eval_list[:, :, None] == corpus_list[:, None, :]) & (
                eval_list[:, :, None] < tiles_slice
            )
            aligned = jnp.einsum(
                "gij,gjrt->girt",
                matched.astype(jnp.bfloat16),
                corpus_part,
                preferred_element_type=jnp.float32,
            ).astype(jnp.bfloat16)
            products = jnp.einsum(
                "girt,gist->grs", eval_part, aligned, preferred_element_type=jnp.float32
            )
            products = jnp.where(living[:, None, None], products, 0.0)
            return lax.dynamic_update_slice_in_dim(current, products, first_slot, 0)

        return lax.cond(jnp.any(living), compute, lambda current: current, totals)

    start_totals = jnp.zeros((pair_slots, tile_rows, tile_rows), jnp.float32)
    summed = lax.psum_scatter(
        lax.fori_loop(0, groups, one_group, start_totals), "vocab", scatter_dimension=0, tiled=True
    )
    first_pair = lax.axis_index("vocab") * quarter
    mine_eval = lax.dynamic_slice_in_dim(pair_eval_block, first_pair, quarter)
    mine_block = lax.dynamic_slice_in_dim(pair_corpus_block, first_pair, quarter)
    mine_live = lax.dynamic_slice_in_dim(own_live, first_pair, quarter)
    eval_scale = eval_norm.reshape(-1, tile_rows)[mine_eval]
    corpus_scale = corpus_norm.reshape(-1, tile_rows)[mine_block]
    cosine = summed / (eval_scale[:, :, None] * corpus_scale[:, None, :])
    return jnp.where(mine_live[:, None, None], cosine, 0.0)


def dots_kernel(tiles_slice, place_ref, eval_list_ref, corpus_list_ref, *refs, arrivals):
    eval_refs, corpus_ref = refs[: len(arrivals)], refs[len(arrivals)]
    keep_ref, send_ref = refs[len(arrivals) + 1 :]
    blocks, slots = corpus_ref.shape[:2]
    half = blocks // 2
    core = place_ref[0]
    for at, (arrival, eval_ref) in enumerate(zip(arrivals, eval_refs)):
        e = place_ref[1 + arrival]
        ids = [eval_list_ref[e, i] for i in range(slots)]
        for side, out_ref in ((0, keep_ref), (1, send_ref)):
            for q in range(half):
                d = ((core + side) % 2) * half + q
                total = None
                for i in range(slots):
                    column, hit = 0, jnp.float32(0.0)
                    for j in range(slots):
                        same = (ids[i] == corpus_list_ref[d, j]) & (ids[i] < tiles_slice)
                        column = jnp.where(same, j, column)
                        hit = jnp.where(same, 1.0, hit)
                    left = eval_ref[0, i] * hit.astype(jnp.bfloat16)
                    product = lax.dot_general(
                        left,
                        corpus_ref[d, column],
                        (((1,), (1,)), ((), ())),
                        preferred_element_type=jnp.float32,
                    )
                    total = product if total is None else total + product
                out_ref[at * half + q] = total


def dots(place, eval_tile_list, corpus_tile_list, corpus_tiles, eval_blocks, arrivals):
    blocks, slots, rows, terms = corpus_tiles.shape
    shape = jax.ShapeDtypeStruct((len(arrivals) * (blocks // 2), rows, rows), jnp.float32)
    return pl.pallas_call(
        functools.partial(dots_kernel, tiles_in_slice(corpus_tiles), arrivals=arrivals),
        out_shape=(shape, shape),
        in_specs=[SMEM] * 3 + [VMEM] * (len(arrivals) + 1),
        out_specs=(VMEM, VMEM),
        compiler_params=pltpu.CompilerParams(vmem_limit_bytes=LIMIT),
        cost_estimate=pl.CostEstimate(
            flops=2 * len(arrivals) * blocks * slots * rows * rows * terms,
            bytes_accessed=2 * (corpus_tiles.size + sum(b.size for b in eval_blocks)),
            transcendentals=0,
        ),
    )(place, eval_tile_list, corpus_tile_list, *eval_blocks, corpus_tiles)


def scale_kernel(eval_ref, corpus_ref, live_ref, out_ref):
    for p in range(out_ref.shape[0]):
        factor = 1.0 / (eval_ref[:, p : p + 1] * corpus_ref[p : p + 1, :])
        out_ref[p] = jnp.where(live_ref[p] > 0, factor, 0.0)


def spread_kernel(chunks, item_ref, scale_ref, *refs):
    sums, (out_ref, table, staged, sem) = refs[:-4], refs[-4:]
    half_items = table.shape[0] // 2
    base = 0
    for t in range(chunks):
        mine, other = sums[2 * t], sums[2 * t + 1]
        n = mine.shape[0]
        table[base : base + n] = mine[...]
        table[half_items + base : half_items + base + n] = other[...]
        base += n
    copies = []
    group = 6 if out_ref.shape[0] % 6 == 0 else out_ref.shape[0]
    for p in range(out_ref.shape[0]):
        staged[p] = table[item_ref[p]] * scale_ref[p]
        if (p + 1) % group == 0:
            part = pl.ds(p + 1 - group, group)
            copy = pltpu.make_async_copy(staged.at[part], out_ref.at[part], sem.at[p // group])
            copy.start()
            copies.append(copy)
    for copy in copies:
        copy.wait()


def few_items(
    eval_tiles,
    eval_tile_list,
    corpus_tiles,
    corpus_tile_list,
    pair_eval_block,
    pair_corpus_block,
    pair_count,
    eval_norm,
    corpus_norm,
):
    shards, slices = lax.axis_size("corpus"), lax.axis_size("vocab")
    rows = corpus_tiles.shape[2]
    blocks = corpus_tiles.shape[0]
    half = blocks // 2
    pair_slots = pair_eval_block.shape[0]
    quarter = pair_slots // slices
    lines = shards // 2

    ring = list(range(0, lines, 2)) + list(range(1, lines, 2))[::-1]
    along = [(ring[i] * 2 + y, ring[(i + 1) % lines] * 2 + y) for i in range(lines) for y in range(2)]
    across = [(c, c ^ 1) for c in range(shards)]
    to_core = [(v, v ^ 1) for v in range(slices)]
    to_chip = [(v, v ^ 2) for v in range(slices)]

    order = [(0, 0)]
    for step in range(1, lines):
        order += [(step, 0), (step - 1, 1)]
    order.append((lines - 1, 1))

    shard, vocab = lax.axis_index("corpus"), lax.axis_index("vocab")
    core = vocab % 2
    ring_at = jnp.asarray(ring, jnp.int32)
    line_of = jnp.arange(lines, dtype=jnp.int32)
    my_ring = jnp.sum(jnp.where(ring_at == shard // 2, line_of, 0))
    steps = jnp.asarray([k for k, _ in order], jnp.int32)
    flips = jnp.asarray([f for _, f in order], jnp.int32)
    from_ring = (my_ring - steps + lines) % lines
    from_line = jnp.sum(jnp.where(from_ring[:, None] == line_of[None, :], ring_at[None, :], 0), axis=1)
    from_shard = from_line * 2 + (shard % 2 ^ flips)
    place = jnp.concatenate([core[None].astype(jnp.int32), from_shard.astype(jnp.int32)])

    first_pair = vocab * quarter
    mine_eval = lax.dynamic_slice_in_dim(pair_eval_block, first_pair, quarter)
    mine_block = lax.dynamic_slice_in_dim(pair_corpus_block, first_pair, quarter)
    arrival_of = jnp.sum(
        jnp.where(mine_eval[:, None] == from_shard[None, :], jnp.arange(shards, dtype=jnp.int32)[None, :], 0), axis=1
    )
    other_side = (mine_block // half) ^ core
    item = other_side * (shards * half) + arrival_of * half + mine_block % half
    live = ((first_pair + jnp.arange(quarter, dtype=jnp.int32)) < pair_count[0]).astype(jnp.int32)
    eval_scale = jnp.sum(
        jnp.where(
            mine_eval[None, :, None] == jnp.arange(shards, dtype=jnp.int32)[None, None, :],
            eval_norm.reshape(shards, rows).T[:, None, :],
            0.0,
        ),
        axis=2,
    )
    corpus_scale = jnp.sum(
        jnp.where(
            mine_block[:, None, None] == jnp.arange(blocks, dtype=jnp.int32)[None, :, None],
            corpus_norm.reshape(blocks, rows)[None],
            0.0,
        ),
        axis=1,
    )
    scale = pl.pallas_call(
        scale_kernel,
        out_shape=jax.ShapeDtypeStruct((quarter, rows, rows), jnp.float32),
        in_specs=[VMEM, VMEM, SMEM],
        out_specs=VMEM,
        compiler_params=pltpu.CompilerParams(vmem_limit_bytes=LIMIT),
    )(eval_scale, corpus_scale, live)

    work = functools.partial(dots, place, eval_tile_list, corpus_tile_list, corpus_tiles)

    def reduce(keep, send):
        chip = keep + lax.ppermute(send, "vocab", to_core)
        total = chip + lax.ppermute(chip, "vocab", to_chip)
        return total, lax.ppermute(total, "vocab", to_core)

    held = eval_tiles
    arrived, names = [eval_tiles], [0]
    sums = []
    for step in range(lines):
        exchanged = lax.ppermute(held, "corpus", across)
        if step < lines - 1:
            moved = lax.ppermute(held, "corpus", along)
            if step > 0:
                sums += reduce(*work(arrived, tuple(names)))
                names = []
                arrived = []
            held, exchanged = lax.optimization_barrier((moved, exchanged))
            names += [1 + 2 * step, 2 + 2 * step]
            arrived += [held, exchanged]
        else:
            sums += reduce(*work(arrived, tuple(names)))
            sums += reduce(*work([exchanged], (2 * lines - 1,)))
    return pl.pallas_call(
        functools.partial(spread_kernel, len(sums) // 2),
        out_shape=jax.ShapeDtypeStruct((quarter, rows, rows), jnp.float32),
        in_specs=[SMEM] + [VMEM] * (1 + len(sums)),
        out_specs=pl.BlockSpec(memory_space=pl.ANY),
        scratch_shapes=[
            pltpu.VMEM((shards * blocks, rows, rows), jnp.float32),
            pltpu.VMEM((quarter, rows, rows), jnp.float32),
            pltpu.SemaphoreType.DMA((quarter,)),
        ],
        compiler_params=pltpu.CompilerParams(vmem_limit_bytes=LIMIT),
    )(item, scale, *sums)


def solution(mesh):
    in_specs = (
        P("corpus", "vocab", None, None),
        P(None, "vocab"),
        P("corpus", "vocab", None, None),
        P("corpus", "vocab"),
        P("corpus"),
        P("corpus"),
        P("corpus"),
        P(),
        P("corpus"),
    )
    out_specs = P(("corpus", "vocab"), None, None)

    def program(*arrays):
        shards, slices = mesh.shape["corpus"], mesh.shape["vocab"]
        evals, blocks, slots = arrays[0].shape[0], arrays[2].shape[0] // shards, arrays[4].shape[0] // shards
        few = slices == 4 and shards == evals and shards % 2 == 0 and blocks % 2 == 0 and evals * blocks <= slots
        local = few_items if few else general
        return jax.shard_map(local, mesh=mesh, in_specs=in_specs, out_specs=out_specs, check_vma=False)(*arrays)

    return program
```

```python
import functools

import jax
import jax.numpy as jnp
from jax import lax
from jax.experimental import pallas as pl
from jax.experimental.pallas import tpu as pltpu
from jax.sharding import PartitionSpec as P

VOCAB = 262144
GROUP = 8
VMEM = pl.BlockSpec(memory_space=pltpu.VMEM)
SMEM = pl.BlockSpec(memory_space=pltpu.SMEM)
LIMIT = 24 * 1024 * 1024
TOP = 32767.0
SCALE_ROWS = 16


def tiles_in_slice(corpus_tiles):
    return VOCAB // (corpus_tiles.shape[3] * lax.axis_size("vocab"))


def general(
    eval_tiles,
    eval_tile_list,
    corpus_tiles,
    corpus_tile_list,
    pair_eval_block,
    pair_corpus_block,
    pair_count,
    eval_norm,
    corpus_norm,
):
    slices = lax.axis_size("vocab")
    tile_rows = corpus_tiles.shape[2]
    tiles_slice = tiles_in_slice(corpus_tiles)
    pair_slots = pair_eval_block.shape[0]
    quarter = pair_slots // slices
    every_eval = lax.all_gather(eval_tiles, "corpus", axis=0, tiled=True)
    position = jnp.arange(pair_slots, dtype=jnp.int32)
    own_live = position < pair_count[0]
    groups = pair_slots // GROUP

    def one_group(group_index, totals):
        first_slot = group_index * GROUP
        living = lax.dynamic_slice_in_dim(own_live, first_slot, GROUP)

        def compute(current):
            eval_index = lax.dynamic_slice_in_dim(pair_eval_block, first_slot, GROUP)
            block_index = lax.dynamic_slice_in_dim(pair_corpus_block, first_slot, GROUP)
            eval_part = every_eval[eval_index]
            eval_list = eval_tile_list[eval_index]
            corpus_part = corpus_tiles[block_index]
            corpus_list = corpus_tile_list[block_index]
            matched = (eval_list[:, :, None] == corpus_list[:, None, :]) & (
                eval_list[:, :, None] < tiles_slice
            )
            aligned = jnp.einsum(
                "gij,gjrt->girt",
                matched.astype(jnp.bfloat16),
                corpus_part,
                preferred_element_type=jnp.float32,
            ).astype(jnp.bfloat16)
            products = jnp.einsum(
                "girt,gist->grs", eval_part, aligned, preferred_element_type=jnp.float32
            )
            products = jnp.where(living[:, None, None], products, 0.0)
            return lax.dynamic_update_slice_in_dim(current, products, first_slot, 0)

        return lax.cond(jnp.any(living), compute, lambda current: current, totals)

    start_totals = jnp.zeros((pair_slots, tile_rows, tile_rows), jnp.float32)
    summed = lax.psum_scatter(
        lax.fori_loop(0, groups, one_group, start_totals), "vocab", scatter_dimension=0, tiled=True
    )
    first_pair = lax.axis_index("vocab") * quarter
    mine_eval = lax.dynamic_slice_in_dim(pair_eval_block, first_pair, quarter)
    mine_block = lax.dynamic_slice_in_dim(pair_corpus_block, first_pair, quarter)
    mine_live = lax.dynamic_slice_in_dim(own_live, first_pair, quarter)
    eval_scale = eval_norm.reshape(-1, tile_rows)[mine_eval]
    corpus_scale = corpus_norm.reshape(-1, tile_rows)[mine_block]
    cosine = summed / (eval_scale[:, :, None] * corpus_scale[:, None, :])
    return jnp.where(mine_live[:, None, None], cosine, 0.0)


def ring_of(shards):
    return list(range(0, shards, 2)) + list(range(1, shards, 2))[::-1]


def look_up(values, at):
    found = jnp.int32(0)
    for n, value in enumerate(values):
        found = jnp.where(at == n, jnp.int32(value), found)
    return found


def ring_place(shards):
    ring = ring_of(shards)
    core = lax.axis_index("vocab") % 2
    return look_up([ring.index(c) for c in range(shards)], lax.axis_index("corpus")), 2 * core - 1, core


def encode(tiles, code_ref):
    rows = tiles[0].shape[0]
    scales = []
    for q, tile in enumerate(tiles):
        scale = jnp.maximum(jnp.ceil(jnp.max(tile, axis=0, keepdims=True) * 2.0), 1.0)
        scales.append(scale)
        whole = jnp.floor(tile * (TOP * 2.0 / scale) + 0.5)
        code_ref[q * rows : (q + 1) * rows] = jnp.minimum(whole, TOP).astype(jnp.int32).astype(jnp.int16)
    scales.append(jnp.zeros((SCALE_ROWS - len(scales), rows), jnp.float32))
    code_ref[len(tiles) * rows :] = jnp.concatenate(scales, axis=0).astype(jnp.int32).astype(jnp.int16)


def decode(code_ref):
    rows = code_ref.shape[1]
    count = code_ref.shape[0] // rows
    scales = code_ref[count * rows :].astype(jnp.int32).astype(jnp.float32) * (0.5 / TOP)
    for q in range(count):
        whole = code_ref[q * rows : (q + 1) * rows].astype(jnp.int32).astype(jnp.float32)
        yield whole * scales[q : q + 1]


def code_shape(count, rows):
    return jax.ShapeDtypeStruct((count * rows + SCALE_ROWS, rows), jnp.int16)


def dots_kernel(tiles_slice, step, halved, carried, coded, *refs):
    outs = len(halved) + coded
    sources = [refs[4 * n : 4 * n + 4] for n in range((len(refs) - outs - carried) // 4)]
    carried_refs = refs[4 * len(sources) : len(refs) - outs]
    out_refs = refs[len(refs) - outs :]
    slots, shards = sources[0][2].shape
    ring = ring_of(shards)
    place, way, core = ring_place(shards)
    e = look_up(ring, (place + way * step + shards) % shards)
    tiles = []
    for out_ref, half in zip(out_refs, halved):
        count = out_ref.shape[0]
        first = 0 if half is None else (core ^ half) * count
        for q in range(count):
            d = first + q
            total = None
            for eval_ref, corpus_ref, eval_ids, corpus_ids in sources:
                for i in range(slots):
                    own = eval_ids[i, e]
                    column, hit = 0, jnp.float32(0.0)
                    for j in range(slots):
                        same = (own == corpus_ids[d, j]) & (own < tiles_slice)
                        column = jnp.where(same, j, column)
                        hit = jnp.where(same, 1.0, hit)
                    product = lax.dot_general(
                        eval_ref[0, i] * hit.astype(jnp.bfloat16),
                        corpus_ref[d, column],
                        (((1,), (1,)), ((), ())),
                        preferred_element_type=jnp.float32,
                    )
                    total = product if total is None else total + product
            out_ref[q] = total
            tiles.append(total)
    if coded:
        encode([ref[q] for ref in carried_refs for q in range(ref.shape[0])] + tiles, out_refs[-1])


def dots(step, sources, halved, carried=(), coded=True):
    blocks, slots, rows, terms = sources[0][1].shape
    counts = [blocks if half is None else blocks // 2 for half in halved]
    outs = [jax.ShapeDtypeStruct((count, rows, rows), jnp.float32) for count in counts]
    if coded:
        outs.append(code_shape(sum(c.shape[0] for c in carried) + counts[0], rows))
    tiles_slice = tiles_in_slice(sources[0][1])
    return pl.pallas_call(
        functools.partial(dots_kernel, tiles_slice, step, halved, len(carried), coded),
        out_shape=tuple(outs),
        in_specs=[VMEM, VMEM, SMEM, SMEM] * len(sources) + [VMEM] * len(carried),
        out_specs=(VMEM,) * len(outs),
        compiler_params=pltpu.CompilerParams(vmem_limit_bytes=LIMIT),
        cost_estimate=pl.CostEstimate(
            flops=2 * sum(counts) * len(sources) * slots * rows * rows * terms,
            bytes_accessed=2 * len(sources) * (blocks + 1) * slots * rows * terms,
            transcendentals=0,
        ),
    )(*[array for source in sources for array in source], *carried)


def add_kernel(near_ref, far_ref, out_ref, code_ref):
    tiles = [near_ref[q] + far_ref[q] for q in range(out_ref.shape[0])]
    for q, tile in enumerate(tiles):
        out_ref[q] = tile
    encode(tiles, code_ref)


def add_and_code(near, far):
    return pl.pallas_call(
        add_kernel,
        out_shape=(jax.ShapeDtypeStruct(near.shape, near.dtype), code_shape(*near.shape[:2])),
        in_specs=[VMEM] * 2,
        out_specs=(VMEM, VMEM),
        compiler_params=pltpu.CompilerParams(vmem_limit_bytes=LIMIT),
    )(near, far)


def joined(parts):
    for *near, code_ref in parts:
        tiles = [ref[q] for ref in near for q in range(ref.shape[0])]
        for tile, there in zip(tiles, decode(code_ref)):
            yield tile + there


def grouped(refs, counts):
    refs = list(refs)
    return [[refs.pop(0) for _ in range(count)] for count in counts]


def join_kernel(counts, *refs):
    *refs, out_ref = refs
    for q, tile in enumerate(joined(grouped(refs, counts))):
        out_ref[q] = tile


def join(parts):
    arrays = [array for part in parts for array in part]
    tiles = [array for part in parts for array in part[:-1]]
    count = sum(array.shape[0] for array in tiles)
    return pl.pallas_call(
        functools.partial(join_kernel, [len(part) for part in parts]),
        out_shape=jax.ShapeDtypeStruct((count, *tiles[0].shape[1:]), jnp.float32),
        in_specs=[VMEM] * len(arrays),
        out_specs=VMEM,
        compiler_params=pltpu.CompilerParams(vmem_limit_bytes=LIMIT),
    )(*arrays)


def load_kernel(count, *refs):
    norms = 2
    arrays = refs[: count + norms]
    copied = refs[count + norms : 2 * count + norms]
    scale_ref, *norm_refs, sem = refs[2 * count + norms :]
    targets = [*copied, *norm_refs]
    copies = [pltpu.make_async_copy(src, dst, sem.at[n]) for n, (src, dst) in enumerate(zip(arrays, targets))]
    for copy in copies:
        copy.start()
    for copy in copies[-norms:]:
        copy.wait()
    eval_norm_ref, corpus_norm_ref = norm_refs
    shards, blocks = eval_norm_ref.shape[0], corpus_norm_ref.shape[0]
    eval_norm = eval_norm_ref[...].T
    for e in range(shards):
        for d in range(blocks):
            scale_ref[e * blocks + d] = 1.0 / (eval_norm[:, e : e + 1] * corpus_norm_ref[d : d + 1, :])
    for copy in copies[:-norms]:
        copy.wait()


def load(arrays, eval_norm, corpus_norm):
    items = eval_norm.shape[0] * corpus_norm.shape[0]
    rows = eval_norm.shape[1]
    given = [pltpu.with_memory_space_constraint(array, pltpu.HBM) for array in (*arrays, eval_norm, corpus_norm)]
    return pl.pallas_call(
        functools.partial(load_kernel, len(arrays)),
        out_shape=[jax.ShapeDtypeStruct(array.shape, array.dtype) for array in arrays]
        + [jax.ShapeDtypeStruct((items, rows, rows), jnp.float32)],
        in_specs=[pl.BlockSpec(memory_space=pltpu.HBM)] * len(given),
        out_specs=[VMEM] * (len(arrays) + 1),
        scratch_shapes=[
            pltpu.VMEM(eval_norm.shape, jnp.float32),
            pltpu.VMEM(corpus_norm.shape, jnp.float32),
            pltpu.SemaphoreType.DMA((len(given),)),
        ],
        compiler_params=pltpu.CompilerParams(vmem_limit_bytes=LIMIT),
    )(*given)


def spread_kernel(shards, blocks, counts, pair_eval_ref, pair_corpus_ref, pair_count_ref, scale_ref, *refs):
    sums, (out_ref, table, staged, sem) = list(refs[:-4]), refs[-4:]
    quarter = out_ref.shape[0]
    ring, far, half = ring_of(shards), shards // 2, blocks // 2
    place, way, core = ring_place(shards)
    for side in range(2):
        early, *late = sums[side * (len(sums) // 2) : (side + 1) * (len(sums) // 2)]
        tiles = [early[q] for q in range(early.shape[0])] + list(joined(grouped(late, counts)))
        at = 0
        for step in range(far + 1):
            e = look_up(ring, (place + (1 - 2 * side) * way * step + shards) % shards)
            shared = step in (0, far)
            for q in range(half if shared else blocks):
                table[e * blocks + ((core ^ side) * half + q if shared else q)] = tiles[at]
                at += 1
    copies = []
    group = 6 if quarter % 6 == 0 else quarter
    for p in range(quarter):
        slot = lax.axis_index("vocab") * quarter + p
        row = pair_eval_ref[slot] * blocks + pair_corpus_ref[slot]
        staged[p] = jnp.where(slot < pair_count_ref[0], table[row] * scale_ref[row], 0.0)
        if (p + 1) % group == 0:
            part = pl.ds(p + 1 - group, group)
            copy = pltpu.make_async_copy(staged.at[part], out_ref.at[part], sem.at[p // group])
            copy.start()
            copies.append(copy)
    for copy in copies:
        copy.wait()


def after(array, *others):
    return lax.optimization_barrier((array, *others))[0]


def few_items(
    eval_tiles,
    eval_tile_list,
    corpus_tiles,
    corpus_tile_list,
    pair_eval_block,
    pair_corpus_block,
    pair_count,
    eval_norm,
    corpus_norm,
):
    shards, slices = lax.axis_size("corpus"), lax.axis_size("vocab")
    blocks, slots, rows = corpus_tiles.shape[:3]
    quarter = pair_eval_block.shape[0] // slices
    far = shards // 2

    ring = ring_of(shards)
    onward = []
    for at in range(shards):
        for v in range(slices):
            to = ring[(at + (1 if v % 2 == 0 else -1)) % shards]
            onward.append((ring[at] * slices + v, to * slices + v))
    to_core = [(v, v ^ 1) for v in range(slices)]
    to_chip = [(v, v ^ 2) for v in range(slices)]

    def move(block):
        return lax.ppermute(block, ("corpus", "vocab"), onward)

    def swap(array):
        return lax.ppermute(array, "vocab", to_core)

    def cross(array):
        return lax.ppermute(array, "vocab", to_chip)

    near, also = [eval_tiles], [swap(eval_tiles)]
    near.append(move(near[0]))
    also.append(move(also[0]))
    corpus_also = swap(corpus_tiles)
    ids = (eval_tile_list.T, corpus_tile_list)
    ids_also = tuple(swap(array) for array in ids)
    given = (corpus_tiles, eval_tiles, *ids, pair_eval_block, pair_corpus_block)
    corpus_tiles, near[0], *ids, pair_eval_block, pair_corpus_block, scale = load(
        given, eval_norm.reshape(shards, rows), corpus_norm.reshape(blocks, rows)
    )
    near[1] = after(near[1], scale)

    def work(step, halved, **more):
        sources = [(near[step], corpus_tiles, *ids)]
        if step < len(also):
            sources.append((also[step], corpus_also, *ids_also))
        return dots(step, sources, halved, **more)

    parts = []
    for step in range(far):
        if step > 0:
            near.append(move(near[step]))
            if step + 1 < far:
                also.append(move(also[step]))
        if step == 0:
            (own,) = work(0, (0,), coded=False)
            also[1] = after(also[1], own)
            continue
        chip, code = work(step, (None,), carried=(own,) if step == 1 else ())
        code_there = cross(code)
        parts.append([own, chip, code_there] if step == 1 else [chip, code_there])
        near[step + 1] = after(near[step + 1], chip)
        if step + 1 < far:
            also[step + 1] = after(also[step + 1], code_there)
    keep, send = work(far, (0, 1), coded=False)
    last, last_code = add_and_code(keep, swap(send))
    parts.append([last, cross(last_code)])
    parts[-3][-1] = after(parts[-3][-1], keep)
    early, late = join(parts[:-2]), parts[-2:]
    mine = [early] + [array for part in late for array in part]
    sums = mine + [swap(array) for array in mine]
    return pl.pallas_call(
        functools.partial(spread_kernel, shards, blocks, [len(part) for part in late]),
        out_shape=jax.ShapeDtypeStruct((quarter, rows, rows), jnp.float32),
        in_specs=[SMEM] * 3 + [VMEM] * (1 + len(sums)),
        out_specs=pl.BlockSpec(memory_space=pl.ANY),
        scratch_shapes=[
            pltpu.VMEM((shards * blocks, rows, rows), jnp.float32),
            pltpu.VMEM((quarter, rows, rows), jnp.float32),
            pltpu.SemaphoreType.DMA((quarter,)),
        ],
        compiler_params=pltpu.CompilerParams(vmem_limit_bytes=LIMIT),
    )(pair_eval_block, pair_corpus_block, pair_count, scale, *sums)


def solution(mesh):
    in_specs = (
        P("corpus", "vocab", None, None),
        P(None, "vocab"),
        P("corpus", "vocab", None, None),
        P("corpus", "vocab"),
        P("corpus"),
        P("corpus"),
        P("corpus"),
        P(),
        P("corpus"),
    )
    out_specs = P(("corpus", "vocab"), None, None)

    def program(*arrays):
        shards, slices = mesh.shape["corpus"], mesh.shape["vocab"]
        evals, blocks, slots = arrays[0].shape[0], arrays[2].shape[0] // shards, arrays[4].shape[0] // shards
        few = slices == 4 and shards == evals and shards % 2 == 0 and blocks % 2 == 0 and evals * blocks <= slots
        local = few_items if few else general
        return jax.shard_map(local, mesh=mesh, in_specs=in_specs, out_specs=out_specs, check_vma=False)(*arrays)

    return program
```

```python
import functools

import jax
import jax.numpy as jnp
from jax import lax
from jax.experimental import pallas as pl
from jax.experimental.pallas import tpu as pltpu
from jax.sharding import PartitionSpec as P

VOCAB = 262144
GROUP = 8
VMEM = pl.BlockSpec(memory_space=pltpu.VMEM)
SMEM = pl.BlockSpec(memory_space=pltpu.SMEM)
LIMIT = 24 * 1024 * 1024
TOP = 32767.0
SCALE_ROWS = 16


def tiles_in_slice(corpus_tiles):
    return VOCAB // (corpus_tiles.shape[3] * lax.axis_size("vocab"))


def general(
    eval_tiles,
    eval_tile_list,
    corpus_tiles,
    corpus_tile_list,
    pair_eval_block,
    pair_corpus_block,
    pair_count,
    eval_norm,
    corpus_norm,
):
    slices = lax.axis_size("vocab")
    tile_rows = corpus_tiles.shape[2]
    tiles_slice = tiles_in_slice(corpus_tiles)
    pair_slots = pair_eval_block.shape[0]
    quarter = pair_slots // slices
    every_eval = lax.all_gather(eval_tiles, "corpus", axis=0, tiled=True)
    position = jnp.arange(pair_slots, dtype=jnp.int32)
    own_live = position < pair_count[0]
    groups = pair_slots // GROUP

    def one_group(group_index, totals):
        first_slot = group_index * GROUP
        living = lax.dynamic_slice_in_dim(own_live, first_slot, GROUP)

        def compute(current):
            eval_index = lax.dynamic_slice_in_dim(pair_eval_block, first_slot, GROUP)
            block_index = lax.dynamic_slice_in_dim(pair_corpus_block, first_slot, GROUP)
            eval_part = every_eval[eval_index]
            eval_list = eval_tile_list[eval_index]
            corpus_part = corpus_tiles[block_index]
            corpus_list = corpus_tile_list[block_index]
            matched = (eval_list[:, :, None] == corpus_list[:, None, :]) & (
                eval_list[:, :, None] < tiles_slice
            )
            aligned = jnp.einsum(
                "gij,gjrt->girt",
                matched.astype(jnp.bfloat16),
                corpus_part,
                preferred_element_type=jnp.float32,
            ).astype(jnp.bfloat16)
            products = jnp.einsum(
                "girt,gist->grs", eval_part, aligned, preferred_element_type=jnp.float32
            )
            products = jnp.where(living[:, None, None], products, 0.0)
            return lax.dynamic_update_slice_in_dim(current, products, first_slot, 0)

        return lax.cond(jnp.any(living), compute, lambda current: current, totals)

    start_totals = jnp.zeros((pair_slots, tile_rows, tile_rows), jnp.float32)
    summed = lax.psum_scatter(
        lax.fori_loop(0, groups, one_group, start_totals), "vocab", scatter_dimension=0, tiled=True
    )
    first_pair = lax.axis_index("vocab") * quarter
    mine_eval = lax.dynamic_slice_in_dim(pair_eval_block, first_pair, quarter)
    mine_block = lax.dynamic_slice_in_dim(pair_corpus_block, first_pair, quarter)
    mine_live = lax.dynamic_slice_in_dim(own_live, first_pair, quarter)
    eval_scale = eval_norm.reshape(-1, tile_rows)[mine_eval]
    corpus_scale = corpus_norm.reshape(-1, tile_rows)[mine_block]
    cosine = summed / (eval_scale[:, :, None] * corpus_scale[:, None, :])
    return jnp.where(mine_live[:, None, None], cosine, 0.0)


def ring_of(shards):
    return list(range(0, shards, 2)) + list(range(1, shards, 2))[::-1]


def look_up(values, at):
    found = jnp.int32(0)
    for n, value in enumerate(values):
        found = jnp.where(at == n, jnp.int32(value), found)
    return found


def ring_place(shards):
    ring = ring_of(shards)
    core = lax.axis_index("vocab") % 2
    return look_up([ring.index(c) for c in range(shards)], lax.axis_index("corpus")), 2 * core - 1, core


def encode(tiles, code_ref):
    rows = tiles[0].shape[0]
    scales = []
    for q, tile in enumerate(tiles):
        scale = jnp.maximum(jnp.ceil(jnp.max(tile, axis=0, keepdims=True) * 2.0), 1.0)
        scales.append(scale)
        whole = jnp.floor(tile * (TOP * 2.0 / scale) + 0.5)
        code_ref[q * rows : (q + 1) * rows] = jnp.minimum(whole, TOP).astype(jnp.int32).astype(jnp.int16)
    scales.append(jnp.zeros((SCALE_ROWS - len(scales), rows), jnp.float32))
    code_ref[len(tiles) * rows :] = jnp.concatenate(scales, axis=0).astype(jnp.int32).astype(jnp.int16)


def decode(code_ref):
    rows = code_ref.shape[1]
    count = code_ref.shape[0] // rows
    scales = code_ref[count * rows :].astype(jnp.int32).astype(jnp.float32) * (0.5 / TOP)
    for q in range(count):
        whole = code_ref[q * rows : (q + 1) * rows].astype(jnp.int32).astype(jnp.float32)
        yield whole * scales[q : q + 1]


def code_shape(count, rows):
    return jax.ShapeDtypeStruct((count * rows + SCALE_ROWS, rows), jnp.int16)


def dots_kernel(tiles_slice, step, halved, carried, coded, *refs):
    outs = 1 + coded
    sources = [refs[4 * n : 4 * n + 4] for n in range((len(refs) - outs - carried) // 4)]
    carried_refs = refs[4 * len(sources) : len(refs) - outs]
    out_ref, *code_ref = refs[len(refs) - outs :]
    slots, shards = sources[0][2].shape
    ring = ring_of(shards)
    place, way, core = ring_place(shards)
    e = look_up(ring, (place + way * step + shards) % shards)
    tiles = []
    count = out_ref.shape[0]
    for q in range(count):
        d = core * count + q if halved else q
        total = None
        for eval_ref, corpus_ref, eval_ids, corpus_ids in sources:
            for i in range(slots):
                own = eval_ids[i, e]
                column, hit = 0, jnp.float32(0.0)
                for j in range(slots):
                    same = (own == corpus_ids[d, j]) & (own < tiles_slice)
                    column = jnp.where(same, j, column)
                    hit = jnp.where(same, 1.0, hit)
                product = lax.dot_general(
                    eval_ref[0, i] * hit.astype(jnp.bfloat16),
                    corpus_ref[d, column],
                    (((1,), (1,)), ((), ())),
                    preferred_element_type=jnp.float32,
                )
                total = product if total is None else total + product
        out_ref[q] = total
        tiles.append(total)
    if coded:
        encode([ref[q] for ref in carried_refs for q in range(ref.shape[0])] + tiles, *code_ref)


def dots(step, sources, halved, carried=(), coded=True):
    blocks, slots, rows, terms = sources[0][1].shape
    count = blocks // 2 if halved else blocks
    outs = [jax.ShapeDtypeStruct((count, rows, rows), jnp.float32)]
    if coded:
        outs.append(code_shape(sum(c.shape[0] for c in carried) + count, rows))
    tiles_slice = tiles_in_slice(sources[0][1])
    return pl.pallas_call(
        functools.partial(dots_kernel, tiles_slice, step, halved, len(carried), coded),
        out_shape=tuple(outs),
        in_specs=[VMEM, VMEM, SMEM, SMEM] * len(sources) + [VMEM] * len(carried),
        out_specs=(VMEM,) * len(outs),
        compiler_params=pltpu.CompilerParams(vmem_limit_bytes=LIMIT),
        cost_estimate=pl.CostEstimate(
            flops=2 * count * len(sources) * slots * rows * rows * terms,
            bytes_accessed=2 * len(sources) * (blocks + 1) * slots * rows * terms,
            transcendentals=0,
        ),
    )(*[array for source in sources for array in source], *carried)


def joined(parts):
    for *near, code_ref in parts:
        tiles = [ref[q] for ref in near for q in range(ref.shape[0])]
        for tile, there in zip(tiles, decode(code_ref)):
            yield tile + there


def grouped(refs, counts):
    refs = list(refs)
    return [[refs.pop(0) for _ in range(count)] for count in counts]


def join_kernel(counts, *refs):
    *refs, out_ref = refs
    for q, tile in enumerate(joined(grouped(refs, counts))):
        out_ref[q] = tile


def join(parts):
    arrays = [array for part in parts for array in part]
    tiles = [array for part in parts for array in part[:-1]]
    count = sum(array.shape[0] for array in tiles)
    return pl.pallas_call(
        functools.partial(join_kernel, [len(part) for part in parts]),
        out_shape=jax.ShapeDtypeStruct((count, *tiles[0].shape[1:]), jnp.float32),
        in_specs=[VMEM] * len(arrays),
        out_specs=VMEM,
        compiler_params=pltpu.CompilerParams(vmem_limit_bytes=LIMIT),
    )(*arrays)


def load_kernel(count, *refs):
    norms = 2
    arrays = refs[: count + norms]
    copied = refs[count + norms : 2 * count + norms]
    scale_ref, *norm_refs, sem = refs[2 * count + norms :]
    targets = [*copied, *norm_refs]
    copies = [pltpu.make_async_copy(src, dst, sem.at[n]) for n, (src, dst) in enumerate(zip(arrays, targets))]
    for copy in copies:
        copy.start()
    for copy in copies[-norms:]:
        copy.wait()
    eval_norm_ref, corpus_norm_ref = norm_refs
    shards, blocks = eval_norm_ref.shape[0], corpus_norm_ref.shape[0]
    eval_norm = eval_norm_ref[...].T
    for e in range(shards):
        for d in range(blocks):
            scale_ref[e * blocks + d] = 1.0 / (eval_norm[:, e : e + 1] * corpus_norm_ref[d : d + 1, :])
    for copy in copies[:-norms]:
        copy.wait()


def load(arrays, eval_norm, corpus_norm):
    items = eval_norm.shape[0] * corpus_norm.shape[0]
    rows = eval_norm.shape[1]
    given = [pltpu.with_memory_space_constraint(array, pltpu.HBM) for array in (*arrays, eval_norm, corpus_norm)]
    return pl.pallas_call(
        functools.partial(load_kernel, len(arrays)),
        out_shape=[jax.ShapeDtypeStruct(array.shape, array.dtype) for array in arrays]
        + [jax.ShapeDtypeStruct((items, rows, rows), jnp.float32)],
        in_specs=[pl.BlockSpec(memory_space=pltpu.HBM)] * len(given),
        out_specs=[VMEM] * (len(arrays) + 1),
        scratch_shapes=[
            pltpu.VMEM(eval_norm.shape, jnp.float32),
            pltpu.VMEM(corpus_norm.shape, jnp.float32),
            pltpu.SemaphoreType.DMA((len(given),)),
        ],
        compiler_params=pltpu.CompilerParams(vmem_limit_bytes=LIMIT),
    )(*given)


def spread_kernel(shards, blocks, counts, pair_eval_ref, pair_corpus_ref, pair_count_ref, scale_ref, *refs):
    sums, (out_ref, table, staged, sem) = list(refs[:-4]), refs[-4:]
    quarter = out_ref.shape[0]
    ring, far, half = ring_of(shards), shards // 2, blocks // 2
    place, way, core = ring_place(shards)
    for side in range(2):
        early, *late = sums[side * (len(sums) // 2) : (side + 1) * (len(sums) // 2)]
        tiles = [early[q] for q in range(early.shape[0])] + list(joined(grouped(late, counts)))
        at = 0
        for step in range(far + 1):
            e = look_up(ring, (place + (1 - 2 * side) * way * step + shards) % shards)
            shared = step in (0, far)
            for q in range(half if shared else blocks):
                table[e * blocks + ((core ^ side) * half + q if shared else q)] = tiles[at]
                at += 1
    copies = []
    group = 6 if quarter % 6 == 0 else quarter
    for p in range(quarter):
        slot = lax.axis_index("vocab") * quarter + p
        row = pair_eval_ref[slot] * blocks + pair_corpus_ref[slot]
        staged[p] = jnp.where(slot < pair_count_ref[0], table[row] * scale_ref[row], 0.0)
        if (p + 1) % group == 0:
            part = pl.ds(p + 1 - group, group)
            copy = pltpu.make_async_copy(staged.at[part], out_ref.at[part], sem.at[p // group])
            copy.start()
            copies.append(copy)
    for copy in copies:
        copy.wait()


def after(array, *others):
    return lax.optimization_barrier((array, *others))[0]


def few_items(
    eval_tiles,
    eval_tile_list,
    corpus_tiles,
    corpus_tile_list,
    pair_eval_block,
    pair_corpus_block,
    pair_count,
    eval_norm,
    corpus_norm,
):
    shards, slices = lax.axis_size("corpus"), lax.axis_size("vocab")
    blocks, slots, rows = corpus_tiles.shape[:3]
    quarter = pair_eval_block.shape[0] // slices
    far = shards // 2

    ring = ring_of(shards)
    onward = []
    for at in range(shards):
        for v in range(slices):
            to = ring[(at + (1 if v % 2 == 0 else -1)) % shards]
            onward.append((ring[at] * slices + v, to * slices + v))
    to_core = [(v, v ^ 1) for v in range(slices)]
    to_chip = [(v, v ^ 2) for v in range(slices)]

    def move(block):
        return lax.ppermute(block, ("corpus", "vocab"), onward)

    def swap(array):
        return lax.ppermute(array, "vocab", to_core)

    def cross(array):
        return lax.ppermute(array, "vocab", to_chip)

    near, also = [eval_tiles], [swap(eval_tiles)]
    near.append(move(near[0]))
    also.append(move(also[0]))
    corpus_also = swap(corpus_tiles)
    ids = (eval_tile_list.T, corpus_tile_list)
    ids_also = tuple(swap(array) for array in ids)
    given = (corpus_tiles, eval_tiles, *ids, pair_eval_block, pair_corpus_block)
    corpus_tiles, near[0], *ids, pair_eval_block, pair_corpus_block, scale = load(
        given, eval_norm.reshape(shards, rows), corpus_norm.reshape(blocks, rows)
    )
    near[1] = after(near[1], scale)

    def work(step, halved, **more):
        sources = [(near[step], corpus_tiles, *ids), (also[step], corpus_also, *ids_also)]
        return dots(step, sources, halved, **more)

    (own,) = work(0, True, coded=False)
    also[1] = after(also[1], own)
    parts = []
    for step in range(1, far):
        near.append(move(near[step]))
        if step + 1 < far:
            also.append(move(also[step]))
        carried = (own,) if step == 1 else ()
        chip, code = work(step, False, carried=carried)
        parts.append([*carried, chip, cross(code)])
        near[step + 1] = after(near[step + 1], chip, *[part[-1] for part in parts[:-1]])
    parts[-2][-1] = after(parts[-2][-1], parts[-1][0])
    early = join(parts[:-1])
    near[far] = after(near[far], early)
    also.append(swap(near[far]))
    last, last_code = work(far, True)
    parts.append([last, cross(last_code)])
    late = parts[-2:]
    mine = [early] + [array for part in late for array in part]
    sums = mine + [swap(array) for array in mine]
    return pl.pallas_call(
        functools.partial(spread_kernel, shards, blocks, [len(part) for part in late]),
        out_shape=jax.ShapeDtypeStruct((quarter, rows, rows), jnp.float32),
        in_specs=[SMEM] * 3 + [VMEM] * (1 + len(sums)),
        out_specs=pl.BlockSpec(memory_space=pl.ANY),
        scratch_shapes=[
            pltpu.VMEM((shards * blocks, rows, rows), jnp.float32),
            pltpu.VMEM((quarter, rows, rows), jnp.float32),
            pltpu.SemaphoreType.DMA((quarter,)),
        ],
        compiler_params=pltpu.CompilerParams(vmem_limit_bytes=LIMIT),
    )(pair_eval_block, pair_corpus_block, pair_count, scale, *sums)


def solution(mesh):
    in_specs = (
        P("corpus", "vocab", None, None),
        P(None, "vocab"),
        P("corpus", "vocab", None, None),
        P("corpus", "vocab"),
        P("corpus"),
        P("corpus"),
        P("corpus"),
        P(),
        P("corpus"),
    )
    out_specs = P(("corpus", "vocab"), None, None)

    def program(*arrays):
        shards, slices = mesh.shape["corpus"], mesh.shape["vocab"]
        evals, blocks, slots = arrays[0].shape[0], arrays[2].shape[0] // shards, arrays[4].shape[0] // shards
        few = slices == 4 and shards == evals and shards % 2 == 0 and blocks % 2 == 0 and evals * blocks <= slots
        local = few_items if few else general
        return jax.shard_map(local, mesh=mesh, in_specs=in_specs, out_specs=out_specs, check_vma=False)(*arrays)

    return program
```

```python
import functools

import jax
import jax.numpy as jnp
from jax import lax
from jax.experimental import pallas as pl
from jax.experimental.pallas import tpu as pltpu
from jax.sharding import PartitionSpec as P

VOCAB = 262144
GROUP = 8
VMEM = pl.BlockSpec(memory_space=pltpu.VMEM)
SMEM = pl.BlockSpec(memory_space=pltpu.SMEM)
LIMIT = 24 * 1024 * 1024
TOP = 32767.0
SCALE_ROWS = 16


def tiles_in_slice(corpus_tiles):
    return VOCAB // (corpus_tiles.shape[3] * lax.axis_size("vocab"))


def general(
    eval_tiles,
    eval_tile_list,
    corpus_tiles,
    corpus_tile_list,
    pair_eval_block,
    pair_corpus_block,
    pair_count,
    eval_norm,
    corpus_norm,
):
    slices = lax.axis_size("vocab")
    tile_rows = corpus_tiles.shape[2]
    tiles_slice = tiles_in_slice(corpus_tiles)
    pair_slots = pair_eval_block.shape[0]
    quarter = pair_slots // slices
    every_eval = lax.all_gather(eval_tiles, "corpus", axis=0, tiled=True)
    position = jnp.arange(pair_slots, dtype=jnp.int32)
    own_live = position < pair_count[0]
    groups = pair_slots // GROUP

    def one_group(group_index, totals):
        first_slot = group_index * GROUP
        living = lax.dynamic_slice_in_dim(own_live, first_slot, GROUP)

        def compute(current):
            eval_index = lax.dynamic_slice_in_dim(pair_eval_block, first_slot, GROUP)
            block_index = lax.dynamic_slice_in_dim(pair_corpus_block, first_slot, GROUP)
            eval_part = every_eval[eval_index]
            eval_list = eval_tile_list[eval_index]
            corpus_part = corpus_tiles[block_index]
            corpus_list = corpus_tile_list[block_index]
            matched = (eval_list[:, :, None] == corpus_list[:, None, :]) & (
                eval_list[:, :, None] < tiles_slice
            )
            aligned = jnp.einsum(
                "gij,gjrt->girt",
                matched.astype(jnp.bfloat16),
                corpus_part,
                preferred_element_type=jnp.float32,
            ).astype(jnp.bfloat16)
            products = jnp.einsum(
                "girt,gist->grs", eval_part, aligned, preferred_element_type=jnp.float32
            )
            products = jnp.where(living[:, None, None], products, 0.0)
            return lax.dynamic_update_slice_in_dim(current, products, first_slot, 0)

        return lax.cond(jnp.any(living), compute, lambda current: current, totals)

    start_totals = jnp.zeros((pair_slots, tile_rows, tile_rows), jnp.float32)
    summed = lax.psum_scatter(
        lax.fori_loop(0, groups, one_group, start_totals), "vocab", scatter_dimension=0, tiled=True
    )
    first_pair = lax.axis_index("vocab") * quarter
    mine_eval = lax.dynamic_slice_in_dim(pair_eval_block, first_pair, quarter)
    mine_block = lax.dynamic_slice_in_dim(pair_corpus_block, first_pair, quarter)
    mine_live = lax.dynamic_slice_in_dim(own_live, first_pair, quarter)
    eval_scale = eval_norm.reshape(-1, tile_rows)[mine_eval]
    corpus_scale = corpus_norm.reshape(-1, tile_rows)[mine_block]
    cosine = summed / (eval_scale[:, :, None] * corpus_scale[:, None, :])
    return jnp.where(mine_live[:, None, None], cosine, 0.0)


def ring_of(shards):
    return list(range(0, shards, 2)) + list(range(1, shards, 2))[::-1]


def look_up(values, at):
    found = jnp.int32(0)
    for n, value in enumerate(values):
        found = jnp.where(at == n, jnp.int32(value), found)
    return found


def ring_place(shards):
    ring = ring_of(shards)
    core = lax.axis_index("vocab") % 2
    return look_up([ring.index(c) for c in range(shards)], lax.axis_index("corpus")), 2 * core - 1, core


def encode(tiles, code_ref):
    rows = tiles[0].shape[0]
    scales = []
    for q, tile in enumerate(tiles):
        scale = jnp.maximum(jnp.ceil(jnp.max(tile, axis=0, keepdims=True) * 2.0), 1.0)
        scales.append(scale)
        whole = jnp.floor(tile * (TOP * 2.0 / scale) + 0.5)
        code_ref[q * rows : (q + 1) * rows] = jnp.minimum(whole, TOP).astype(jnp.int32).astype(jnp.int16)
    scales.append(jnp.zeros((SCALE_ROWS - len(scales), rows), jnp.float32))
    code_ref[len(tiles) * rows :] = jnp.concatenate(scales, axis=0).astype(jnp.int32).astype(jnp.int16)


def decode(code_ref):
    rows = code_ref.shape[1]
    count = code_ref.shape[0] // rows
    scales = code_ref[count * rows :].astype(jnp.int32).astype(jnp.float32) * (0.5 / TOP)
    for q in range(count):
        whole = code_ref[q * rows : (q + 1) * rows].astype(jnp.int32).astype(jnp.float32)
        yield whole * scales[q : q + 1]


def code_shape(count, rows):
    return jax.ShapeDtypeStruct((count * rows + SCALE_ROWS, rows), jnp.int16)


def dots_kernel(tiles_slice, step, halved, carried, coded, *refs):
    outs = 1 + coded
    sources = [refs[4 * n : 4 * n + 4] for n in range((len(refs) - outs - carried) // 4)]
    carried_refs = refs[4 * len(sources) : len(refs) - outs]
    out_ref, *code_ref = refs[len(refs) - outs :]
    slots, shards = sources[0][2].shape
    ring = ring_of(shards)
    place, way, core = ring_place(shards)
    e = look_up(ring, (place + way * step + shards) % shards)
    tiles = []
    count = out_ref.shape[0]
    for q in range(count):
        d = core * count + q if halved else q
        total = None
        for eval_ref, corpus_ref, eval_ids, corpus_ids in sources:
            for i in range(slots):
                own = eval_ids[i, e]
                column, hit = 0, jnp.float32(0.0)
                for j in range(slots):
                    same = (own == corpus_ids[d, j]) & (own < tiles_slice)
                    column = jnp.where(same, j, column)
                    hit = jnp.where(same, 1.0, hit)
                product = lax.dot_general(
                    eval_ref[0, i] * hit.astype(jnp.bfloat16),
                    corpus_ref[d, column],
                    (((1,), (1,)), ((), ())),
                    preferred_element_type=jnp.float32,
                )
                total = product if total is None else total + product
        out_ref[q] = total
        tiles.append(total)
    if coded:
        encode([ref[q] for ref in carried_refs for q in range(ref.shape[0])] + tiles, *code_ref)


def dots(step, sources, halved, carried=(), coded=True):
    blocks, slots, rows, terms = sources[0][1].shape
    count = blocks // 2 if halved else blocks
    outs = [jax.ShapeDtypeStruct((count, rows, rows), jnp.float32)]
    if coded:
        outs.append(code_shape(sum(c.shape[0] for c in carried) + count, rows))
    tiles_slice = tiles_in_slice(sources[0][1])
    return pl.pallas_call(
        functools.partial(dots_kernel, tiles_slice, step, halved, len(carried), coded),
        out_shape=tuple(outs),
        in_specs=[VMEM, VMEM, SMEM, SMEM] * len(sources) + [VMEM] * len(carried),
        out_specs=(VMEM,) * len(outs),
        compiler_params=pltpu.CompilerParams(vmem_limit_bytes=LIMIT),
        cost_estimate=pl.CostEstimate(
            flops=2 * count * len(sources) * slots * rows * rows * terms,
            bytes_accessed=2 * len(sources) * (blocks + 1) * slots * rows * terms,
            transcendentals=0,
        ),
    )(*[array for source in sources for array in source], *carried)


def joined(parts):
    for *near, code_ref in parts:
        tiles = [ref[q] for ref in near for q in range(ref.shape[0])]
        for tile, there in zip(tiles, decode(code_ref)):
            yield tile + there


def grouped(refs, counts):
    refs = list(refs)
    return [[refs.pop(0) for _ in range(count)] for count in counts]


def join_kernel(counts, *refs):
    *refs, out_ref = refs
    for q, tile in enumerate(joined(grouped(refs, counts))):
        out_ref[q] = tile


def join(parts):
    arrays = [array for part in parts for array in part]
    tiles = [array for part in parts for array in part[:-1]]
    count = sum(array.shape[0] for array in tiles)
    return pl.pallas_call(
        functools.partial(join_kernel, [len(part) for part in parts]),
        out_shape=jax.ShapeDtypeStruct((count, *tiles[0].shape[1:]), jnp.float32),
        in_specs=[VMEM] * len(arrays),
        out_specs=VMEM,
        compiler_params=pltpu.CompilerParams(vmem_limit_bytes=LIMIT),
    )(*arrays)


def load_kernel(count, *refs):
    norms = 2
    arrays = refs[: count + norms]
    copied = refs[count + norms : 2 * count + norms]
    scale_ref, *norm_refs, sem = refs[2 * count + norms :]
    targets = [*copied, *norm_refs]
    copies = [pltpu.make_async_copy(src, dst, sem.at[n]) for n, (src, dst) in enumerate(zip(arrays, targets))]
    for copy in copies:
        copy.start()
    for copy in copies[-norms:]:
        copy.wait()
    eval_norm_ref, corpus_norm_ref = norm_refs
    shards, blocks = eval_norm_ref.shape[0], corpus_norm_ref.shape[0]
    eval_norm = eval_norm_ref[...].T
    for e in range(shards):
        for d in range(blocks):
            scale_ref[e * blocks + d] = 1.0 / (eval_norm[:, e : e + 1] * corpus_norm_ref[d : d + 1, :])
    for copy in copies[:-norms]:
        copy.wait()


def load(arrays, eval_norm, corpus_norm):
    items = eval_norm.shape[0] * corpus_norm.shape[0]
    rows = eval_norm.shape[1]
    given = [pltpu.with_memory_space_constraint(array, pltpu.HBM) for array in (*arrays, eval_norm, corpus_norm)]
    return pl.pallas_call(
        functools.partial(load_kernel, len(arrays)),
        out_shape=[jax.ShapeDtypeStruct(array.shape, array.dtype) for array in arrays]
        + [jax.ShapeDtypeStruct((items, rows, rows), jnp.float32)],
        in_specs=[pl.BlockSpec(memory_space=pltpu.HBM)] * len(given),
        out_specs=[VMEM] * (len(arrays) + 1),
        scratch_shapes=[
            pltpu.VMEM(eval_norm.shape, jnp.float32),
            pltpu.VMEM(corpus_norm.shape, jnp.float32),
            pltpu.SemaphoreType.DMA((len(given),)),
        ],
        compiler_params=pltpu.CompilerParams(vmem_limit_bytes=LIMIT),
    )(*given)


def steps_of(shards, blocks, side, steps):
    ring, far, half = ring_of(shards), shards // 2, blocks // 2
    place, way, core = ring_place(shards)
    for step in steps:
        e = look_up(ring, (place + (1 - 2 * side) * way * step + shards) % shards)
        shared = step in (0, far)
        for q in range(half if shared else blocks):
            yield e, (core ^ side) * half + q if shared else q


def rows_of(blocks, pair_eval_ref, pair_corpus_ref, quarter):
    for p in range(quarter):
        slot = lax.axis_index("vocab") * quarter + p
        yield p, slot, pair_eval_ref[slot], pair_eval_ref[slot] * blocks + pair_corpus_ref[slot]


def comes_late(shards, e):
    ring, far = ring_of(shards), shards // 2
    place, _, _ = ring_place(shards)
    at = look_up([ring.index(c) for c in range(shards)], e)
    distance = (at - place + shards) % shards
    return (distance >= far - 1) & (distance <= far + 1)


def table_kernel(shards, blocks, scale_ref, mine_ref, other_ref, table_ref):
    for side, sums_ref in enumerate((mine_ref, other_ref)):
        for at, (e, d) in enumerate(steps_of(shards, blocks, side, range(shards // 2 - 1))):
            row = e * blocks + d
            table_ref[row] = sums_ref[at] * scale_ref[row]


def spread_kernel(shards, blocks, counts, pair_eval_ref, pair_corpus_ref, pair_count_ref, scale_ref, early_ref, *refs):
    *sums, out_ref, table, zeros, sem = refs
    quarter = out_ref.shape[0]
    half = len(sums) // 2
    zeros[...] = jnp.zeros_like(zeros)
    slots = []
    for p, slot, e, row in rows_of(blocks, pair_eval_ref, pair_corpus_ref, quarter):
        live, late = slot < pair_count_ref[0], comes_late(shards, e)
        slots.append((p, row, live & late))
        pl.when(live & jnp.logical_not(late))(pltpu.make_async_copy(early_ref.at[row], out_ref.at[p], sem.at[p]).start)
        pl.when(jnp.logical_not(live))(pltpu.make_async_copy(zeros, out_ref.at[p], sem.at[p]).start)
    for side in range(2):
        tiles = joined(grouped(sums[side * half : (side + 1) * half], counts))
        for tile, (e, d) in zip(tiles, steps_of(shards, blocks, side, (shards // 2 - 1, shards // 2))):
            table[e * blocks + d] = tile * scale_ref[e * blocks + d]
    for p, row, late in slots:
        pl.when(late)(pltpu.make_async_copy(table.at[row], out_ref.at[p], sem.at[p]).start)
    for p in range(quarter):
        pltpu.make_async_copy(zeros, out_ref.at[p], sem.at[p]).wait()


def after(array, *others):
    return lax.optimization_barrier((array, *others))[0]


def few_items(
    eval_tiles,
    eval_tile_list,
    corpus_tiles,
    corpus_tile_list,
    pair_eval_block,
    pair_corpus_block,
    pair_count,
    eval_norm,
    corpus_norm,
):
    shards, slices = lax.axis_size("corpus"), lax.axis_size("vocab")
    blocks, slots, rows = corpus_tiles.shape[:3]
    quarter = pair_eval_block.shape[0] // slices
    far = shards // 2

    ring = ring_of(shards)
    onward = []
    for at in range(shards):
        for v in range(slices):
            to = ring[(at + (1 if v % 2 == 0 else -1)) % shards]
            onward.append((ring[at] * slices + v, to * slices + v))
    to_core = [(v, v ^ 1) for v in range(slices)]
    to_chip = [(v, v ^ 2) for v in range(slices)]

    def move(block):
        return lax.ppermute(block, ("corpus", "vocab"), onward)

    def swap(array):
        return lax.ppermute(array, "vocab", to_core)

    def cross(array):
        return lax.ppermute(array, "vocab", to_chip)

    near, also = [eval_tiles], [swap(eval_tiles)]
    near.append(move(near[0]))
    also.append(move(also[0]))
    corpus_also = swap(corpus_tiles)
    ids = (eval_tile_list.T, corpus_tile_list)
    ids_also = tuple(swap(array) for array in ids)
    given = (corpus_tiles, eval_tiles, *ids, pair_eval_block, pair_corpus_block)
    corpus_tiles, near[0], *ids, pair_eval_block, pair_corpus_block, scale = load(
        given, eval_norm.reshape(shards, rows), corpus_norm.reshape(blocks, rows)
    )
    near[1] = after(near[1], scale)

    def work(step, halved, **more):
        sources = [(near[step], corpus_tiles, *ids), (also[step], corpus_also, *ids_also)]
        return dots(step, sources, halved, **more)

    (own,) = work(0, True, coded=False)
    also[1] = after(also[1], own)
    parts = []
    for step in range(1, far):
        near.append(move(near[step]))
        if step + 1 < far:
            also.append(move(also[step]))
        carried = (own,) if step == 1 else ()
        chip, code = work(step, False, carried=carried)
        parts.append([*carried, chip, cross(code)])
        near[step + 1] = after(near[step + 1], chip, *[part[-1] for part in parts[:-1]])
    parts[-2][-1] = after(parts[-2][-1], parts[-1][0])
    early = join(parts[:-1])
    near[far] = after(near[far], early)
    also.append(swap(near[far]))
    last, last_code = work(far, True)
    parts.append([last, cross(last_code)])
    late = parts[-2:]
    early_other = swap(early)
    table = jax.ShapeDtypeStruct((shards * blocks, rows, rows), jnp.float32)
    cosines = pl.pallas_call(
        functools.partial(table_kernel, shards, blocks),
        out_shape=table,
        in_specs=[VMEM] * 3,
        out_specs=VMEM,
        compiler_params=pltpu.CompilerParams(vmem_limit_bytes=LIMIT),
    )(scale, early, early_other)
    mine = [array for part in late for array in part]
    sums = mine + [swap(array) for array in mine]
    return pl.pallas_call(
        functools.partial(spread_kernel, shards, blocks, [len(part) for part in late]),
        out_shape=jax.ShapeDtypeStruct((quarter, rows, rows), jnp.float32),
        in_specs=[SMEM] * 3 + [VMEM] * (2 + len(sums)),
        out_specs=pl.BlockSpec(memory_space=pl.ANY),
        scratch_shapes=[
            pltpu.VMEM(table.shape, jnp.float32),
            pltpu.VMEM((rows, rows), jnp.float32),
            pltpu.SemaphoreType.DMA((quarter,)),
        ],
        compiler_params=pltpu.CompilerParams(vmem_limit_bytes=LIMIT),
    )(pair_eval_block, pair_corpus_block, pair_count, scale, cosines, *sums)


def solution(mesh):
    in_specs = (
        P("corpus", "vocab", None, None),
        P(None, "vocab"),
        P("corpus", "vocab", None, None),
        P("corpus", "vocab"),
        P("corpus"),
        P("corpus"),
        P("corpus"),
        P(),
        P("corpus"),
    )
    out_specs = P(("corpus", "vocab"), None, None)

    def program(*arrays):
        shards, slices = mesh.shape["corpus"], mesh.shape["vocab"]
        evals, blocks, slots = arrays[0].shape[0], arrays[2].shape[0] // shards, arrays[4].shape[0] // shards
        few = slices == 4 and shards == evals and shards % 2 == 0 and blocks % 2 == 0 and evals * blocks <= slots
        local = few_items if few else general
        return jax.shard_map(local, mesh=mesh, in_specs=in_specs, out_specs=out_specs, check_vma=False)(*arrays)

    return program
```

```python
import functools

import jax
import jax.numpy as jnp
from jax import lax
from jax.experimental import pallas as pl
from jax.experimental.pallas import tpu as pltpu
from jax.sharding import PartitionSpec as P

VOCAB = 262144
GROUP = 8
VMEM = pl.BlockSpec(memory_space=pltpu.VMEM)
SMEM = pl.BlockSpec(memory_space=pltpu.SMEM)
LIMIT = 24 * 1024 * 1024
TOP = 32767.0
SCALE_ROWS = 16


def tiles_in_slice(corpus_tiles):
    return VOCAB // (corpus_tiles.shape[3] * lax.axis_size("vocab"))


def general(
    eval_tiles,
    eval_tile_list,
    corpus_tiles,
    corpus_tile_list,
    pair_eval_block,
    pair_corpus_block,
    pair_count,
    eval_norm,
    corpus_norm,
):
    slices = lax.axis_size("vocab")
    tile_rows = corpus_tiles.shape[2]
    tiles_slice = tiles_in_slice(corpus_tiles)
    pair_slots = pair_eval_block.shape[0]
    quarter = pair_slots // slices
    every_eval = lax.all_gather(eval_tiles, "corpus", axis=0, tiled=True)
    position = jnp.arange(pair_slots, dtype=jnp.int32)
    own_live = position < pair_count[0]
    groups = pair_slots // GROUP

    def one_group(group_index, totals):
        first_slot = group_index * GROUP
        living = lax.dynamic_slice_in_dim(own_live, first_slot, GROUP)

        def compute(current):
            eval_index = lax.dynamic_slice_in_dim(pair_eval_block, first_slot, GROUP)
            block_index = lax.dynamic_slice_in_dim(pair_corpus_block, first_slot, GROUP)
            eval_part = every_eval[eval_index]
            eval_list = eval_tile_list[eval_index]
            corpus_part = corpus_tiles[block_index]
            corpus_list = corpus_tile_list[block_index]
            matched = (eval_list[:, :, None] == corpus_list[:, None, :]) & (
                eval_list[:, :, None] < tiles_slice
            )
            aligned = jnp.einsum(
                "gij,gjrt->girt",
                matched.astype(jnp.bfloat16),
                corpus_part,
                preferred_element_type=jnp.float32,
            ).astype(jnp.bfloat16)
            products = jnp.einsum(
                "girt,gist->grs", eval_part, aligned, preferred_element_type=jnp.float32
            )
            products = jnp.where(living[:, None, None], products, 0.0)
            return lax.dynamic_update_slice_in_dim(current, products, first_slot, 0)

        return lax.cond(jnp.any(living), compute, lambda current: current, totals)

    start_totals = jnp.zeros((pair_slots, tile_rows, tile_rows), jnp.float32)
    summed = lax.psum_scatter(
        lax.fori_loop(0, groups, one_group, start_totals), "vocab", scatter_dimension=0, tiled=True
    )
    first_pair = lax.axis_index("vocab") * quarter
    mine_eval = lax.dynamic_slice_in_dim(pair_eval_block, first_pair, quarter)
    mine_block = lax.dynamic_slice_in_dim(pair_corpus_block, first_pair, quarter)
    mine_live = lax.dynamic_slice_in_dim(own_live, first_pair, quarter)
    eval_scale = eval_norm.reshape(-1, tile_rows)[mine_eval]
    corpus_scale = corpus_norm.reshape(-1, tile_rows)[mine_block]
    cosine = summed / (eval_scale[:, :, None] * corpus_scale[:, None, :])
    return jnp.where(mine_live[:, None, None], cosine, 0.0)


def ring_of(shards):
    return list(range(0, shards, 2)) + list(range(1, shards, 2))[::-1]


def look_up(values, at):
    found = jnp.int32(0)
    for n, value in enumerate(values):
        found = jnp.where(at == n, jnp.int32(value), found)
    return found


def ring_place(shards):
    ring = ring_of(shards)
    core = lax.axis_index("vocab") % 2
    return look_up([ring.index(c) for c in range(shards)], lax.axis_index("corpus")), 2 * core - 1, core


def encode(tiles, code_ref):
    rows = tiles[0].shape[0]
    scales = []
    for q, tile in enumerate(tiles):
        scale = jnp.maximum(jnp.ceil(jnp.max(tile, axis=0, keepdims=True) * 2.0), 1.0)
        scales.append(scale)
        whole = jnp.floor(tile * (TOP * 2.0 / scale) + 0.5)
        code_ref[q * rows : (q + 1) * rows] = jnp.minimum(whole, TOP).astype(jnp.int32).astype(jnp.int16)
    scales.append(jnp.zeros((SCALE_ROWS - len(scales), rows), jnp.float32))
    code_ref[len(tiles) * rows :] = jnp.concatenate(scales, axis=0).astype(jnp.int32).astype(jnp.int16)


def decode(code_ref):
    rows = code_ref.shape[1]
    count = code_ref.shape[0] // rows
    scales = code_ref[count * rows :].astype(jnp.int32).astype(jnp.float32) * (0.5 / TOP)
    for q in range(count):
        whole = code_ref[q * rows : (q + 1) * rows].astype(jnp.int32).astype(jnp.float32)
        yield whole * scales[q : q + 1]


def code_shape(count, rows):
    return jax.ShapeDtypeStruct((count * rows + SCALE_ROWS, rows), jnp.int16)


def dots_kernel(tiles_slice, step, halved, carried, coded, *refs):
    outs = 1 + coded
    sources = [refs[4 * n : 4 * n + 4] for n in range((len(refs) - outs - carried) // 4)]
    carried_refs = refs[4 * len(sources) : len(refs) - outs]
    out_ref, *code_ref = refs[len(refs) - outs :]
    slots, shards = sources[0][2].shape
    ring = ring_of(shards)
    place, way, core = ring_place(shards)
    e = look_up(ring, (place + way * step + shards) % shards)
    tiles = []
    count = out_ref.shape[0]
    for q in range(count):
        d = core * count + q if halved else q
        total = None
        for eval_ref, corpus_ref, eval_ids, corpus_ids in sources:
            for i in range(slots):
                own = eval_ids[i, e]
                column, hit = 0, jnp.float32(0.0)
                for j in range(slots):
                    same = (own == corpus_ids[d, j]) & (own < tiles_slice)
                    column = jnp.where(same, j, column)
                    hit = jnp.where(same, 1.0, hit)
                product = lax.dot_general(
                    eval_ref[0, i] * hit.astype(jnp.bfloat16),
                    corpus_ref[d, column],
                    (((1,), (1,)), ((), ())),
                    preferred_element_type=jnp.float32,
                )
                total = product if total is None else total + product
        out_ref[q] = total
        tiles.append(total)
    if coded:
        encode([ref[q] for ref in carried_refs for q in range(ref.shape[0])] + tiles, *code_ref)


def dots(step, sources, halved, carried=(), coded=True):
    blocks, slots, rows, terms = sources[0][1].shape
    count = blocks // 2 if halved else blocks
    outs = [jax.ShapeDtypeStruct((count, rows, rows), jnp.float32)]
    if coded:
        outs.append(code_shape(sum(c.shape[0] for c in carried) + count, rows))
    tiles_slice = tiles_in_slice(sources[0][1])
    return pl.pallas_call(
        functools.partial(dots_kernel, tiles_slice, step, halved, len(carried), coded),
        out_shape=tuple(outs),
        in_specs=[VMEM, VMEM, SMEM, SMEM] * len(sources) + [VMEM] * len(carried),
        out_specs=(VMEM,) * len(outs),
        compiler_params=pltpu.CompilerParams(vmem_limit_bytes=LIMIT),
        cost_estimate=pl.CostEstimate(
            flops=2 * count * len(sources) * slots * rows * rows * terms,
            bytes_accessed=2 * len(sources) * (blocks + 1) * slots * rows * terms,
            transcendentals=0,
        ),
    )(*[array for source in sources for array in source], *carried)


def joined(parts):
    for *near, code_ref in parts:
        tiles = [ref[q] for ref in near for q in range(ref.shape[0])]
        for tile, there in zip(tiles, decode(code_ref)):
            yield tile + there


def grouped(refs, counts):
    refs = list(refs)
    return [[refs.pop(0) for _ in range(count)] for count in counts]


def join_kernel(shards, blocks, counts, pair_eval_ref, pair_corpus_ref, pair_count_ref, *refs):
    *refs, out_ref, slot_ref = refs
    for q, tile in enumerate(joined(grouped(refs, counts))):
        out_ref[q] = tile
    quarter = slot_ref.shape[0]
    for p in range(quarter):
        slot = lax.axis_index("vocab") * quarter + p
        row = pair_eval_ref[slot] * blocks + pair_corpus_ref[slot]
        slot_ref[p] = jnp.where(slot < pair_count_ref[0], row, shards * blocks)


def join(shards, blocks, quarter, pairs, parts):
    arrays = [array for part in parts for array in part]
    tiles = [array for part in parts for array in part[:-1]]
    count = sum(array.shape[0] for array in tiles)
    return pl.pallas_call(
        functools.partial(join_kernel, shards, blocks, [len(part) for part in parts]),
        out_shape=(
            jax.ShapeDtypeStruct((count, *tiles[0].shape[1:]), jnp.float32),
            jax.ShapeDtypeStruct((quarter,), jnp.int32),
        ),
        in_specs=[SMEM] * 3 + [VMEM] * len(arrays),
        out_specs=(VMEM, SMEM),
        compiler_params=pltpu.CompilerParams(vmem_limit_bytes=LIMIT),
    )(*pairs, *arrays)


def load_kernel(count, *refs):
    norms = 2
    arrays = refs[: count + norms]
    copied = refs[count + norms : 2 * count + norms]
    scale_ref, *norm_refs, sem = refs[2 * count + norms :]
    targets = [*copied, *norm_refs]
    copies = [pltpu.make_async_copy(src, dst, sem.at[n]) for n, (src, dst) in enumerate(zip(arrays, targets))]
    for copy in copies:
        copy.start()
    for copy in copies[-norms:]:
        copy.wait()
    eval_norm_ref, corpus_norm_ref = norm_refs
    shards, blocks = eval_norm_ref.shape[0], corpus_norm_ref.shape[0]
    eval_norm = eval_norm_ref[...].T
    for e in range(shards):
        for d in range(blocks):
            scale_ref[e * blocks + d] = 1.0 / (eval_norm[:, e : e + 1] * corpus_norm_ref[d : d + 1, :])
    for copy in copies[:-norms]:
        copy.wait()


def load(arrays, eval_norm, corpus_norm):
    items = eval_norm.shape[0] * corpus_norm.shape[0]
    rows = eval_norm.shape[1]
    given = [pltpu.with_memory_space_constraint(array, pltpu.HBM) for array in (*arrays, eval_norm, corpus_norm)]
    return pl.pallas_call(
        functools.partial(load_kernel, len(arrays)),
        out_shape=[jax.ShapeDtypeStruct(array.shape, array.dtype) for array in arrays]
        + [jax.ShapeDtypeStruct((items, rows, rows), jnp.float32)],
        in_specs=[pl.BlockSpec(memory_space=pltpu.HBM)] * len(given),
        out_specs=[VMEM] * (len(arrays) + 1),
        scratch_shapes=[
            pltpu.VMEM(eval_norm.shape, jnp.float32),
            pltpu.VMEM(corpus_norm.shape, jnp.float32),
            pltpu.SemaphoreType.DMA((len(given),)),
        ],
        compiler_params=pltpu.CompilerParams(vmem_limit_bytes=LIMIT),
    )(*given)


def steps_of(shards, blocks, side, steps):
    ring, far, half = ring_of(shards), shards // 2, blocks // 2
    place, way, core = ring_place(shards)
    for step in steps:
        e = look_up(ring, (place + (1 - 2 * side) * way * step + shards) % shards)
        shared = step in (0, far)
        for q in range(half if shared else blocks):
            yield e, (core ^ side) * half + q if shared else q


def table_kernel(shards, blocks, scale_ref, mine_ref, other_ref, table_ref):
    for side, sums_ref in enumerate((mine_ref, other_ref)):
        for at, (e, d) in enumerate(steps_of(shards, blocks, side, range(shards // 2 - 1))):
            table_ref[e * blocks + d] = sums_ref[at] * scale_ref[e * blocks + d]
    table_ref[shards * blocks] = jnp.zeros(table_ref.shape[1:], jnp.float32)


def spread_kernel(shards, blocks, counts, slot_ref, scale_ref, *refs):
    *sums, _, table_ref, out_ref, row_ref, row_sem, sem = refs
    half = len(sums) // 2
    rows_copy = pltpu.make_async_copy(slot_ref, row_ref, row_sem)
    rows_copy.start()
    for side in range(2):
        tiles = joined(grouped(sums[side * half : (side + 1) * half], counts))
        for tile, (e, d) in zip(tiles, steps_of(shards, blocks, side, (shards // 2 - 1, shards // 2))):
            table_ref[e * blocks + d] = tile * scale_ref[e * blocks + d]
    rows_copy.wait()
    for p in range(out_ref.shape[0]):
        pltpu.make_async_copy(table_ref.at[row_ref[p]], out_ref.at[p], sem).start()
    pltpu.make_async_copy(out_ref, out_ref, sem).wait()


def after(array, *others):
    return lax.optimization_barrier((array, *others))[0]


def few_items(
    eval_tiles,
    eval_tile_list,
    corpus_tiles,
    corpus_tile_list,
    pair_eval_block,
    pair_corpus_block,
    pair_count,
    eval_norm,
    corpus_norm,
):
    shards, slices = lax.axis_size("corpus"), lax.axis_size("vocab")
    blocks, slots, rows = corpus_tiles.shape[:3]
    quarter = pair_eval_block.shape[0] // slices
    far = shards // 2

    ring = ring_of(shards)
    onward = []
    for at in range(shards):
        for v in range(slices):
            to = ring[(at + (1 if v % 2 == 0 else -1)) % shards]
            onward.append((ring[at] * slices + v, to * slices + v))
    to_core = [(v, v ^ 1) for v in range(slices)]
    to_chip = [(v, v ^ 2) for v in range(slices)]

    def move(block):
        return lax.ppermute(block, ("corpus", "vocab"), onward)

    def swap(array):
        return lax.ppermute(array, "vocab", to_core)

    def cross(array):
        return lax.ppermute(array, "vocab", to_chip)

    near, also = [eval_tiles], [swap(eval_tiles)]
    near.append(move(near[0]))
    also.append(move(also[0]))
    corpus_also = swap(corpus_tiles)
    ids = (eval_tile_list.T, corpus_tile_list)
    ids_also = tuple(swap(array) for array in ids)
    given = (corpus_tiles, eval_tiles, *ids, pair_eval_block, pair_corpus_block)
    corpus_tiles, near[0], *ids, pair_eval_block, pair_corpus_block, scale = load(
        given, eval_norm.reshape(shards, rows), corpus_norm.reshape(blocks, rows)
    )
    near[1] = after(near[1], scale)

    def work(step, halved, **more):
        sources = [(near[step], corpus_tiles, *ids), (also[step], corpus_also, *ids_also)]
        return dots(step, sources, halved, **more)

    (own,) = work(0, True, coded=False)
    also[1] = after(also[1], own)
    parts = []
    for step in range(1, far):
        near.append(move(near[step]))
        if step + 1 < far:
            also.append(move(also[step]))
        carried = (own,) if step == 1 else ()
        chip, code = work(step, False, carried=carried)
        parts.append([*carried, chip, cross(code)])
        near[step + 1] = after(near[step + 1], chip, *[part[-1] for part in parts[:-1]])
    parts[-2][-1] = after(parts[-2][-1], parts[-1][0])
    pairs = (pair_eval_block, pair_corpus_block, pair_count)
    early, slot_rows = join(shards, blocks, quarter, pairs, parts[:-1])
    near[far] = after(near[far], early)
    also.append(swap(near[far]))
    last, last_code = work(far, True)
    parts.append([last, cross(last_code)])
    late = parts[-2:]
    early_other = swap(early)
    table = jax.ShapeDtypeStruct((shards * blocks + 1, rows, rows), jnp.float32)
    cosines = pl.pallas_call(
        functools.partial(table_kernel, shards, blocks),
        out_shape=table,
        in_specs=[VMEM] * 3,
        out_specs=VMEM,
        compiler_params=pltpu.CompilerParams(vmem_limit_bytes=LIMIT),
    )(scale, early, early_other)
    mine = [array for part in late for array in part]
    sums = mine + [swap(array) for array in mine]
    return pl.pallas_call(
        functools.partial(spread_kernel, shards, blocks, [len(part) for part in late]),
        out_shape=(table, jax.ShapeDtypeStruct((quarter, rows, rows), jnp.float32)),
        in_specs=[VMEM] * (3 + len(sums)),
        out_specs=(VMEM, pl.BlockSpec(memory_space=pl.ANY)),
        input_output_aliases={2 + len(sums): 0},
        scratch_shapes=[pltpu.SMEM((quarter,), jnp.int32), pltpu.SemaphoreType.DMA, pltpu.SemaphoreType.DMA],
        compiler_params=pltpu.CompilerParams(vmem_limit_bytes=LIMIT),
    )(slot_rows, scale, *sums, cosines)[1]


def solution(mesh):
    in_specs = (
        P("corpus", "vocab", None, None),
        P(None, "vocab"),
        P("corpus", "vocab", None, None),
        P("corpus", "vocab"),
        P("corpus"),
        P("corpus"),
        P("corpus"),
        P(),
        P("corpus"),
    )
    out_specs = P(("corpus", "vocab"), None, None)

    def program(*arrays):
        shards, slices = mesh.shape["corpus"], mesh.shape["vocab"]
        evals, blocks, slots = arrays[0].shape[0], arrays[2].shape[0] // shards, arrays[4].shape[0] // shards
        few = slices == 4 and shards == evals and shards % 2 == 0 and blocks % 2 == 0 and evals * blocks <= slots
        local = few_items if few else general
        return jax.shard_map(local, mesh=mesh, in_specs=in_specs, out_specs=out_specs, check_vma=False)(*arrays)

    return program
```

```python
import functools

import jax
import jax.numpy as jnp
from jax import lax
from jax.experimental import pallas as pl
from jax.experimental.pallas import tpu as pltpu
from jax.sharding import PartitionSpec as P

VOCAB = 262144
GROUP = 8
VMEM = pl.BlockSpec(memory_space=pltpu.VMEM)
SMEM = pl.BlockSpec(memory_space=pltpu.SMEM)
LIMIT = 24 * 1024 * 1024
TOP = 32767.0
SCALE_ROWS = 16


def tiles_in_slice(corpus_tiles):
    return VOCAB // (corpus_tiles.shape[3] * lax.axis_size("vocab"))


def general(
    eval_tiles,
    eval_tile_list,
    corpus_tiles,
    corpus_tile_list,
    pair_eval_block,
    pair_corpus_block,
    pair_count,
    eval_norm,
    corpus_norm,
):
    slices = lax.axis_size("vocab")
    tile_rows = corpus_tiles.shape[2]
    tiles_slice = tiles_in_slice(corpus_tiles)
    pair_slots = pair_eval_block.shape[0]
    quarter = pair_slots // slices
    every_eval = lax.all_gather(eval_tiles, "corpus", axis=0, tiled=True)
    position = jnp.arange(pair_slots, dtype=jnp.int32)
    own_live = position < pair_count[0]
    groups = pair_slots // GROUP

    def one_group(group_index, totals):
        first_slot = group_index * GROUP
        living = lax.dynamic_slice_in_dim(own_live, first_slot, GROUP)

        def compute(current):
            eval_index = lax.dynamic_slice_in_dim(pair_eval_block, first_slot, GROUP)
            block_index = lax.dynamic_slice_in_dim(pair_corpus_block, first_slot, GROUP)
            eval_part = every_eval[eval_index]
            eval_list = eval_tile_list[eval_index]
            corpus_part = corpus_tiles[block_index]
            corpus_list = corpus_tile_list[block_index]
            matched = (eval_list[:, :, None] == corpus_list[:, None, :]) & (
                eval_list[:, :, None] < tiles_slice
            )
            aligned = jnp.einsum(
                "gij,gjrt->girt",
                matched.astype(jnp.bfloat16),
                corpus_part,
                preferred_element_type=jnp.float32,
            ).astype(jnp.bfloat16)
            products = jnp.einsum(
                "girt,gist->grs", eval_part, aligned, preferred_element_type=jnp.float32
            )
            products = jnp.where(living[:, None, None], products, 0.0)
            return lax.dynamic_update_slice_in_dim(current, products, first_slot, 0)

        return lax.cond(jnp.any(living), compute, lambda current: current, totals)

    start_totals = jnp.zeros((pair_slots, tile_rows, tile_rows), jnp.float32)
    summed = lax.psum_scatter(
        lax.fori_loop(0, groups, one_group, start_totals), "vocab", scatter_dimension=0, tiled=True
    )
    first_pair = lax.axis_index("vocab") * quarter
    mine_eval = lax.dynamic_slice_in_dim(pair_eval_block, first_pair, quarter)
    mine_block = lax.dynamic_slice_in_dim(pair_corpus_block, first_pair, quarter)
    mine_live = lax.dynamic_slice_in_dim(own_live, first_pair, quarter)
    eval_scale = eval_norm.reshape(-1, tile_rows)[mine_eval]
    corpus_scale = corpus_norm.reshape(-1, tile_rows)[mine_block]
    cosine = summed / (eval_scale[:, :, None] * corpus_scale[:, None, :])
    return jnp.where(mine_live[:, None, None], cosine, 0.0)


def ring_of(shards):
    return list(range(0, shards, 2)) + list(range(1, shards, 2))[::-1]


def look_up(values, at):
    found = jnp.int32(0)
    for n, value in enumerate(values):
        found = jnp.where(at == n, jnp.int32(value), found)
    return found


def ring_place(shards):
    ring = ring_of(shards)
    core = lax.axis_index("vocab") % 2
    return look_up([ring.index(c) for c in range(shards)], lax.axis_index("corpus")), 2 * core - 1, core


def encode(tiles, code_ref):
    rows = tiles[0].shape[0]
    scales = []
    for q, tile in enumerate(tiles):
        scale = jnp.maximum(jnp.ceil(jnp.max(tile, axis=0, keepdims=True) * 2.0), 1.0)
        scales.append(scale)
        whole = jnp.floor(tile * (TOP * 2.0 / scale) + 0.5)
        code_ref[q * rows : (q + 1) * rows] = jnp.minimum(whole, TOP).astype(jnp.int32).astype(jnp.int16)
    scales.append(jnp.zeros((SCALE_ROWS - len(scales), rows), jnp.float32))
    code_ref[len(tiles) * rows :] = jnp.concatenate(scales, axis=0).astype(jnp.int32).astype(jnp.int16)


def decode(code_ref):
    rows = code_ref.shape[1]
    count = code_ref.shape[0] // rows
    scales = code_ref[count * rows :].astype(jnp.int32).astype(jnp.float32) * (0.5 / TOP)
    for q in range(count):
        whole = code_ref[q * rows : (q + 1) * rows].astype(jnp.int32).astype(jnp.float32)
        yield whole * scales[q : q + 1]


def code_shape(count, rows):
    return jax.ShapeDtypeStruct((count * rows + SCALE_ROWS, rows), jnp.int16)


def dots_kernel(tiles_slice, step, halved, carried, coded, *refs):
    outs = 1 + coded
    sources = [refs[4 * n : 4 * n + 4] for n in range((len(refs) - outs - carried) // 4)]
    carried_refs = refs[4 * len(sources) : len(refs) - outs]
    out_ref, *code_ref = refs[len(refs) - outs :]
    slots, shards = sources[0][2].shape
    ring = ring_of(shards)
    place, way, core = ring_place(shards)
    e = look_up(ring, (place + way * step + shards) % shards)
    tiles = []
    count = out_ref.shape[0]
    for q in range(count):
        d = core * count + q if halved else q
        total = None
        for eval_ref, corpus_ref, eval_ids, corpus_ids in sources:
            for i in range(slots):
                own = eval_ids[i, e]
                column, hit = 0, jnp.float32(0.0)
                for j in range(slots):
                    same = (own == corpus_ids[d, j]) & (own < tiles_slice)
                    column = jnp.where(same, j, column)
                    hit = jnp.where(same, 1.0, hit)
                product = lax.dot_general(
                    eval_ref[0, i] * hit.astype(jnp.bfloat16),
                    corpus_ref[d, column],
                    (((1,), (1,)), ((), ())),
                    preferred_element_type=jnp.float32,
                )
                total = product if total is None else total + product
        out_ref[q] = total
        tiles.append(total)
    if coded:
        encode([ref[q] for ref in carried_refs for q in range(ref.shape[0])] + tiles, *code_ref)


def dots(step, sources, halved, carried=(), coded=True):
    blocks, slots, rows, terms = sources[0][1].shape
    count = blocks // 2 if halved else blocks
    outs = [jax.ShapeDtypeStruct((count, rows, rows), jnp.float32)]
    if coded:
        outs.append(code_shape(sum(c.shape[0] for c in carried) + count, rows))
    tiles_slice = tiles_in_slice(sources[0][1])
    return pl.pallas_call(
        functools.partial(dots_kernel, tiles_slice, step, halved, len(carried), coded),
        out_shape=tuple(outs),
        in_specs=[VMEM, VMEM, SMEM, SMEM] * len(sources) + [VMEM] * len(carried),
        out_specs=(VMEM,) * len(outs),
        compiler_params=pltpu.CompilerParams(vmem_limit_bytes=LIMIT),
        cost_estimate=pl.CostEstimate(
            flops=2 * count * len(sources) * slots * rows * rows * terms,
            bytes_accessed=2 * len(sources) * (blocks + 1) * slots * rows * terms,
            transcendentals=0,
        ),
    )(*[array for source in sources for array in source], *carried)


def joined(parts):
    for *near, code_ref in parts:
        tiles = [ref[q] for ref in near for q in range(ref.shape[0])]
        for tile, there in zip(tiles, decode(code_ref)):
            yield tile + there


def grouped(refs, counts):
    refs = list(refs)
    return [[refs.pop(0) for _ in range(count)] for count in counts]


def join_kernel(counts, *refs):
    *refs, out_ref = refs
    for q, tile in enumerate(joined(grouped(refs, counts))):
        out_ref[q] = tile


def join(parts):
    arrays = [array for part in parts for array in part]
    tiles = [array for part in parts for array in part[:-1]]
    count = sum(array.shape[0] for array in tiles)
    return pl.pallas_call(
        functools.partial(join_kernel, [len(part) for part in parts]),
        out_shape=jax.ShapeDtypeStruct((count, *tiles[0].shape[1:]), jnp.float32),
        in_specs=[VMEM] * len(arrays),
        out_specs=VMEM,
        compiler_params=pltpu.CompilerParams(vmem_limit_bytes=LIMIT),
    )(*arrays)


def load_kernel(count, *refs):
    given, pair_count_ref = refs[: count + 4], refs[count + 4]
    copied, rest = refs[count + 5 : 2 * count + 5], refs[2 * count + 5 :]
    scale_ref, slot_ref, eval_norm_ref, corpus_norm_ref, pair_eval_ref, pair_corpus_ref, sem = rest
    targets = [*copied, eval_norm_ref, corpus_norm_ref, pair_eval_ref, pair_corpus_ref]
    copies = [pltpu.make_async_copy(src, dst, sem.at[n]) for n, (src, dst) in enumerate(zip(given, targets))]
    for copy in copies:
        copy.start()
    for copy in copies[count:]:
        copy.wait()
    shards, blocks = eval_norm_ref.shape[0], corpus_norm_ref.shape[0]
    eval_norm = eval_norm_ref[...].T
    for e in range(shards):
        for d in range(blocks):
            scale_ref[e * blocks + d] = 1.0 / (eval_norm[:, e : e + 1] * corpus_norm_ref[d : d + 1, :])
    quarter = slot_ref.shape[0]
    for p in range(quarter):
        slot = lax.axis_index("vocab") * quarter + p
        row = pair_eval_ref[slot] * blocks + pair_corpus_ref[slot]
        slot_ref[p] = jnp.where(slot < pair_count_ref[0], row, shards * blocks)
    for copy in copies[:count]:
        copy.wait()


def load(arrays, norms, pairs, pair_count, quarter):
    items = norms[0].shape[0] * norms[1].shape[0]
    rows = norms[0].shape[1]
    given = [pltpu.with_memory_space_constraint(array, pltpu.HBM) for array in (*arrays, *norms, *pairs)]
    return pl.pallas_call(
        functools.partial(load_kernel, len(arrays)),
        out_shape=[jax.ShapeDtypeStruct(array.shape, array.dtype) for array in arrays]
        + [jax.ShapeDtypeStruct((items, rows, rows), jnp.float32), jax.ShapeDtypeStruct((quarter,), jnp.int32)],
        in_specs=[pl.BlockSpec(memory_space=pltpu.HBM)] * len(given) + [SMEM],
        out_specs=[VMEM] * (len(arrays) + 1) + [SMEM],
        scratch_shapes=[pltpu.VMEM(norm.shape, norm.dtype) for norm in norms]
        + [pltpu.SMEM(array.shape, array.dtype) for array in pairs]
        + [pltpu.SemaphoreType.DMA((len(given),))],
        compiler_params=pltpu.CompilerParams(vmem_limit_bytes=LIMIT),
    )(*given, pair_count)


def steps_of(shards, blocks, side, steps):
    ring, far, half = ring_of(shards), shards // 2, blocks // 2
    place, way, core = ring_place(shards)
    for step in steps:
        e = look_up(ring, (place + (1 - 2 * side) * way * step + shards) % shards)
        shared = step in (0, far)
        for q in range(half if shared else blocks):
            yield e, (core ^ side) * half + q if shared else q


def table_kernel(shards, blocks, scale_ref, mine_ref, other_ref, table_ref):
    for side, sums_ref in enumerate((mine_ref, other_ref)):
        for at, (e, d) in enumerate(steps_of(shards, blocks, side, range(shards // 2 - 1))):
            table_ref[e * blocks + d] = sums_ref[at] * scale_ref[e * blocks + d]
    table_ref[shards * blocks] = jnp.zeros(table_ref.shape[1:], jnp.float32)


def spread_kernel(shards, blocks, counts, slot_ref, scale_ref, *refs):
    *sums, _, table_ref, out_ref, row_ref, row_sem, sem = refs
    half = len(sums) // 2
    rows_copy = pltpu.make_async_copy(slot_ref, row_ref, row_sem)
    rows_copy.start()
    for side in range(2):
        tiles = joined(grouped(sums[side * half : (side + 1) * half], counts))
        for tile, (e, d) in zip(tiles, steps_of(shards, blocks, side, (shards // 2 - 1, shards // 2))):
            table_ref[e * blocks + d] = tile * scale_ref[e * blocks + d]
    rows_copy.wait()
    for p in range(out_ref.shape[0]):
        pltpu.make_async_copy(table_ref.at[row_ref[p]], out_ref.at[p], sem).start()
    pltpu.make_async_copy(out_ref, out_ref, sem).wait()


def after(array, *others):
    return lax.optimization_barrier((array, *others))[0]


def few_items(
    eval_tiles,
    eval_tile_list,
    corpus_tiles,
    corpus_tile_list,
    pair_eval_block,
    pair_corpus_block,
    pair_count,
    eval_norm,
    corpus_norm,
):
    shards, slices = lax.axis_size("corpus"), lax.axis_size("vocab")
    blocks, slots, rows = corpus_tiles.shape[:3]
    quarter = pair_eval_block.shape[0] // slices
    far = shards // 2

    ring = ring_of(shards)
    onward = []
    for at in range(shards):
        for v in range(slices):
            to = ring[(at + (1 if v % 2 == 0 else -1)) % shards]
            onward.append((ring[at] * slices + v, to * slices + v))
    to_core = [(v, v ^ 1) for v in range(slices)]
    to_chip = [(v, v ^ 2) for v in range(slices)]

    def move(block):
        return lax.ppermute(block, ("corpus", "vocab"), onward)

    def swap(array):
        return lax.ppermute(array, "vocab", to_core)

    def cross(array):
        return lax.ppermute(array, "vocab", to_chip)

    near, also = [eval_tiles], [swap(eval_tiles)]
    near.append(move(near[0]))
    also.append(move(also[0]))
    corpus_also = swap(corpus_tiles)
    ids = (eval_tile_list.T, corpus_tile_list)
    ids_also = tuple(swap(array) for array in ids)
    corpus_tiles, near[0], *ids, scale, slot_rows = load(
        (corpus_tiles, eval_tiles, *ids),
        (eval_norm.reshape(shards, rows), corpus_norm.reshape(blocks, rows)),
        (pair_eval_block, pair_corpus_block),
        pair_count,
        quarter,
    )
    near[1] = after(near[1], scale)

    def work(step, halved, **more):
        sources = [(near[step], corpus_tiles, *ids), (also[step], corpus_also, *ids_also)]
        return dots(step, sources, halved, **more)

    (own,) = work(0, True, coded=False)
    also[1] = after(also[1], own)
    parts = []
    for step in range(1, far):
        near.append(move(near[step]))
        if step + 1 < far:
            also.append(move(also[step]))
        carried = (own,) if step == 1 else ()
        chip, code = work(step, False, carried=carried)
        parts.append([*carried, chip, cross(code)])
        near[step + 1] = after(near[step + 1], chip, *[part[-1] for part in parts[:-1]])
    parts[-2][-1] = after(parts[-2][-1], parts[-1][0])
    early = join(parts[:-1])
    near[far] = after(near[far], early)
    also.append(swap(near[far]))
    last, last_code = work(far, True)
    parts.append([last, cross(last_code)])
    late = parts[-2:]
    early_other = swap(early)
    table = jax.ShapeDtypeStruct((shards * blocks + 1, rows, rows), jnp.float32)
    cosines = pl.pallas_call(
        functools.partial(table_kernel, shards, blocks),
        out_shape=table,
        in_specs=[VMEM] * 3,
        out_specs=VMEM,
        compiler_params=pltpu.CompilerParams(vmem_limit_bytes=LIMIT),
    )(scale, early, early_other)
    mine = [array for part in late for array in part]
    sums = mine + [swap(array) for array in mine]
    return pl.pallas_call(
        functools.partial(spread_kernel, shards, blocks, [len(part) for part in late]),
        out_shape=(table, jax.ShapeDtypeStruct((quarter, rows, rows), jnp.float32)),
        in_specs=[VMEM] * (3 + len(sums)),
        out_specs=(VMEM, pl.BlockSpec(memory_space=pl.ANY)),
        input_output_aliases={2 + len(sums): 0},
        scratch_shapes=[pltpu.SMEM((quarter,), jnp.int32), pltpu.SemaphoreType.DMA, pltpu.SemaphoreType.DMA],
        compiler_params=pltpu.CompilerParams(vmem_limit_bytes=LIMIT),
    )(slot_rows, scale, *sums, cosines)[1]


def solution(mesh):
    in_specs = (
        P("corpus", "vocab", None, None),
        P(None, "vocab"),
        P("corpus", "vocab", None, None),
        P("corpus", "vocab"),
        P("corpus"),
        P("corpus"),
        P("corpus"),
        P(),
        P("corpus"),
    )
    out_specs = P(("corpus", "vocab"), None, None)

    def program(*arrays):
        shards, slices = mesh.shape["corpus"], mesh.shape["vocab"]
        evals, blocks, slots = arrays[0].shape[0], arrays[2].shape[0] // shards, arrays[4].shape[0] // shards
        few = slices == 4 and shards == evals and shards % 2 == 0 and blocks % 2 == 0 and evals * blocks <= slots
        local = few_items if few else general
        return jax.shard_map(local, mesh=mesh, in_specs=in_specs, out_specs=out_specs, check_vma=False)(*arrays)

    return program
```
